32 devices in a mesh: section: 4 (over y, x), ctx: 8 (over z, core).
Axes of the slice: x: 2, y: 2, z: 4, core: 2. Of those that a mesh axis runs over, the one named last changes fastest.
Arguments:
- projected: bfloat16 [4, 3072, 3072], P('section', 'ctx'), may hold values from -64 to 64
- grad_out: bfloat16 [4, 3072, 3072], P('section', 'ctx'), may hold values from -6 to 6
- doc_lengths: int32 [7], replicated, may hold values from 1 to 768, as said below
Outputs:
- grad_kv: float32 [3072, 2048], P('ctx')
The draws below stay inside these ranges and needn't reach their ends.
Inputs may be any that keep to these rules, and one draw needn't show every extreme that they name: `doc_lengths`: the lengths sum to 3072; the first document is shorter than 384 tokens and the second has exactly 768.
All inputs are finite; a program needn't handle non-finite values.
Results may differ from the reference program's by a relative error of at most 0.0031.
Values may be sent and summed in bfloat16 or wider, within the bound.
A program may use at most 128 MiB of HBM per device.

```python
import math
import jax
import jax.numpy as jnp
from jax import lax

HEAD_SIZE = 128
KV_HEAD_COUNT = 8
QUERY_PER_KV = 3
QUERY_HEADS = 24
BLOCK_TOKENS = 384
SECTIONS = 4
WINDOW_TOKENS = 3072
DOC_MAX = 768
DOCS = 7


def draw_projected(key, part):
    block_offset = jnp.clip(jax.random.normal(key, (SECTIONS, WINDOW_TOKENS, QUERY_HEADS * HEAD_SIZE), jnp.float32), -6.0, 6.0)
    return block_offset.astype(jnp.bfloat16)


def draw_doc_lengths(key, part):
    key_first, key_pairs = jax.random.split(jax.random.fold_in(key, 23))
    first_len = jax.random.randint(key_first, (1,), 1, BLOCK_TOKENS, jnp.int32)
    pair_count = (DOCS - 3) // 2
    offsets = jax.random.randint(key_pairs, (pair_count,), -(BLOCK_TOKENS - 1), BLOCK_TOKENS, jnp.int32)
    paired = jnp.stack([BLOCK_TOKENS + offsets, BLOCK_TOKENS - offsets], axis=1).reshape(-1)
    longest = jnp.full((1,), DOC_MAX, jnp.int32)
    closing = 2 * BLOCK_TOKENS - first_len
    return jnp.concatenate([first_len, longest, paired.astype(jnp.int32), closing]).astype(jnp.int32)


def shard_levels(rng, extent, shards, smallest, high):
    factor_of = 1.0
    for dim, shards_of in shards:
        heights = jax.random.uniform(jax.random.fold_in(jax.random.fold_in(rng, 6), dim), (shards_of,), jnp.float32, smallest / len(shards), high / len(shards))
        factor_of = factor_of * jnp.repeat(jnp.exp(heights), extent[dim] // shards_of).reshape((-1,) + (1,) * (len(extent) - 1 - dim))
    return factor_of


def gaussian(rng, shape, deviation, limit, pieces=(), kind=jnp.bfloat16):
    gain = shard_levels(rng, shape, pieces, -0.22, 0.18) if pieces else 1.0
    result = jax.random.normal(rng, shape, jnp.float32) * deviation * gain
    return jnp.minimum(jnp.maximum(result, -limit), limit).astype(kind)


def setup_inputs(seed: int = 0) -> dict:
    key_of = jax.random.split(jax.random.key(seed), 4)
    return {
        "projected": draw_projected(jax.random.fold_in(key_of[3], 71), 0),
        "grad_out": gaussian(key_of[1], (SECTIONS, WINDOW_TOKENS, QUERY_HEADS * HEAD_SIZE), 1.0, 6.0, ((0, 4), (1, 8))),
        "doc_lengths": draw_doc_lengths(jax.random.fold_in(key_of[3], 71), 0),
    }


MASKED_SCORE = -1e+30

def document_of(places, doc_ends):
    return lax.optimization_barrier(jnp.sum((doc_ends[None, :] <= places[:, None]).astype(jnp.int32), axis=1)).astype(jnp.int32)

def reference(projected, grad_out, doc_lengths):
    section_count = projected.shape[0]
    shared_width = KV_HEAD_COUNT * HEAD_SIZE
    out_width = 2 * shared_width
    span_row_count = DOC_MAX + BLOCK_TOKENS
    score_scale = 1.0 / math.sqrt(HEAD_SIZE)
    highest = lax.Precision.HIGHEST
    doc_ends = jnp.cumsum(doc_lengths).astype(jnp.int32)
    padded = jnp.concatenate([jnp.zeros((DOC_MAX, out_width), projected.dtype), projected[0][:, :out_width]], axis=0).astype(jnp.float32)
    key_full = padded[:, :shared_width]
    value_full = padded[:, shared_width:]
    summed = jnp.zeros((DOC_MAX + WINDOW_TOKENS, out_width), jnp.float32)
    for section_index in range(1, section_count):
        query_full = projected[section_index].astype(jnp.float32)
        gradient_full = grad_out[section_index].astype(jnp.float32)

        def step_block(block_index, accum):
            first_row = (block_index * BLOCK_TOKENS).astype(jnp.int32)
            query_slice = lax.dynamic_slice_in_dim(query_full, first_row, BLOCK_TOKENS, 0).reshape(BLOCK_TOKENS, KV_HEAD_COUNT, QUERY_PER_KV, HEAD_SIZE)
            gradient_rows = lax.dynamic_slice_in_dim(gradient_full, first_row, BLOCK_TOKENS, 0).reshape(BLOCK_TOKENS, KV_HEAD_COUNT, QUERY_PER_KV, HEAD_SIZE)
            key_slice = lax.dynamic_slice_in_dim(key_full, first_row, span_row_count, 0).reshape(span_row_count, KV_HEAD_COUNT, HEAD_SIZE)
            value_slice = lax.dynamic_slice_in_dim(value_full, first_row, span_row_count, 0).reshape(span_row_count, KV_HEAD_COUNT, HEAD_SIZE)
            query_place = first_row + jnp.arange(BLOCK_TOKENS, dtype=jnp.int32)
            key_place = first_row - DOC_MAX + jnp.arange(span_row_count, dtype=jnp.int32)
            same_doc = document_of(query_place, doc_ends)[:, None] == document_of(key_place, doc_ends)[None, :]
            allowed = same_doc & (key_place[None, :] <= query_place[:, None]) & (key_place[None, :] >= 0)
            scores = jnp.einsum('qgah,kgh->gaqk', query_slice, key_slice, precision=highest) * score_scale
            scores = jnp.where(allowed[None, None], scores, MASKED_SCORE)
            row_top = lax.optimization_barrier(jnp.max(scores, axis=3, keepdims=True))
            powers = jnp.exp(scores - row_top)
            attn_weight = powers / lax.optimization_barrier(jnp.sum(powers, axis=3, keepdims=True))
            attn_half = lax.optimization_barrier(attn_weight.astype(jnp.bfloat16)).astype(jnp.float32)
            attended = jnp.einsum('gaqk,kgh->qgah', attn_half, value_slice, precision=highest)
            delta_rows = jnp.transpose(lax.optimization_barrier(jnp.sum(gradient_rows * attended, axis=3)), (1, 2, 0))
            grad_prob = jnp.einsum('qgah,kgh->gaqk', gradient_rows, value_slice, precision=highest)
            grad_score = attn_weight * (grad_prob - delta_rows[..., None])
            grad_score = lax.optimization_barrier(grad_score.astype(jnp.bfloat16)).astype(jnp.float32)
            grad_key = jnp.einsum('gaqk,qgah->kgh', grad_score, query_slice, precision=highest) * score_scale
            grad_value = jnp.einsum('gaqk,qgah->kgh', attn_half, gradient_rows, precision=highest)
            update = jnp.concatenate([grad_key.reshape(span_row_count, shared_width), grad_value.reshape(span_row_count, shared_width)], axis=1)
            current = lax.dynamic_slice_in_dim(accum, first_row, span_row_count, 0)
            return lax.dynamic_update_slice_in_dim(accum, current + update, first_row, 0)
        summed = lax.fori_loop(0, WINDOW_TOKENS // BLOCK_TOKENS, step_block, summed)
    return summed[DOC_MAX:]
```

```python
import functools
import math

import jax
import jax.numpy as jnp
from jax import lax
from jax.experimental import pallas as pl
from jax.experimental.pallas import tpu as pltpu
from jax.sharding import PartitionSpec as P

HEAD_SIZE = 128
KV_HEAD_COUNT = 8
QUERY_PER_KV = 3
REACH = 2
ROWS = 128
AHEAD = 3
MASKED_SCORE = -1e30
MESH = pl.DeviceIdType.MESH


def ring_swap(place, sections):
    half = sections // 2
    back = place // half
    return place * (1 - back) + back * (half + sections - 1 - place)


def dot_last(left, right):
    return lax.dot_general(
        left, right, (((1,), (1,)), ((), ())), preferred_element_type=jnp.float32
    )


def folded(value, reduce):
    return reduce(value.reshape(-1, 8, value.shape[-1]), axis=0)


def kernel(
    sections,
    blocks,
    lengths_ref,
    projected_ref,
    grad_out_ref,
    out_ref,
    queries,
    cotangents,
    window,
    bias,
    score_buf,
    prob_grad_buf,
    grads,
    pair_in,
    hop_out,
    hop_in,
    part_out,
    part_in,
    final,
    load_sem,
    ring_send,
    ring_recv,
    hop_kv_send,
    hop_kv_recv,
    pair_kv_send,
    pair_kv_recv,
    pair_send,
    pair_recv,
    hop_send,
    hop_recv,
    part_send,
    part_recv,
    spread_send,
    spread_recv,
    store_sem,
):
    section = lax.axis_index("section")
    block = lax.axis_index("ctx")
    odd = lax.rem(block, 2)
    partner = block + 1 - 2 * odd
    place = ring_swap(section, sections)
    heads = KV_HEAD_COUNT
    tokens = out_ref.shape[0]
    width = heads * HEAD_SIZE
    group_width = QUERY_PER_KV * HEAD_SIZE
    span = REACH * tokens + ROWS
    scale = 1.0 / math.sqrt(HEAD_SIZE)
    exponent_scale = scale * math.log2(math.e)
    cross = section > 0
    has_before = block >= REACH
    has_after = block + REACH < blocks

    def block_rows(index):
        return pl.ds(index * tokens, tokens)

    def load_shared(head, kind):
        return pltpu.make_async_copy(
            projected_ref.at[:, pl.ds(kind * width + head * HEAD_SIZE, HEAD_SIZE)],
            window.at[head, kind, block_rows(REACH), :],
            load_sem.at[head, kind],
        )

    def load_group(head, kind):
        source, target = ((projected_ref, queries), (grad_out_ref, cotangents))[kind]
        return pltpu.make_async_copy(
            source.at[:, pl.ds(head * group_width, group_width)],
            target.at[head],
            load_sem.at[head, kind],
        )

    def ring_copy(head, kind):
        target_place = lax.rem(place + 1 - 2 * kind + sections, sections)
        own = window.at[head, kind, block_rows(REACH), :]
        return pltpu.make_async_remote_copy(
            src_ref=own,
            dst_ref=own,
            send_sem=ring_send.at[head, kind],
            recv_sem=ring_recv.at[head, kind],
            device_id={"section": ring_swap(target_place, sections), "ctx": block},
            device_id_type=MESH,
        )

    def ring_goes_on(kind):
        return lax.rem(place + 1 - 2 * kind + sections, sections) != 0

    def to_block(source, target, send_sem, recv_sem, target_block):
        return pltpu.make_async_remote_copy(
            src_ref=source,
            dst_ref=target,
            send_sem=send_sem,
            recv_sem=recv_sem,
            device_id={"section": section, "ctx": target_block},
            device_id_type=MESH,
        )

    def hop_kv(head):
        return to_block(
            window.at[head, :, block_rows(REACH), :],
            window.at[head, :, block_rows(0), :],
            hop_kv_send.at[head],
            hop_kv_recv.at[head],
            block + REACH,
        )

    def pair_kv(head, source_block):
        return to_block(
            window.at[head, :, block_rows(source_block), :],
            window.at[head, :, block_rows(1), :],
            pair_kv_send.at[head],
            pair_kv_recv.at[head],
            partner,
        )

    def pair_grads(head):
        return to_block(
            grads.at[head, :, block_rows(1), :],
            pair_in.at[head],
            pair_send.at[head],
            pair_recv.at[head],
            partner,
        )

    def hop_grads(head):
        return to_block(
            hop_out.at[head], hop_in.at[head], hop_send.at[head], hop_recv.at[head], block - REACH
        )

    def part_copy(head, source, target):
        return pltpu.make_async_remote_copy(
            src_ref=part_out.at[head],
            dst_ref=part_in.at[head // sections, source],
            send_sem=part_send.at[head],
            recv_sem=part_recv.at[head // sections, source],
            device_id={"section": target, "ctx": block},
            device_id_type=MESH,
        )

    def out_columns(head, kind):
        start = pl.multiple_of(kind * width + head * HEAD_SIZE, HEAD_SIZE)
        return out_ref.at[:, pl.ds(start, HEAD_SIZE)]

    def spread_copy(head, kind, target):
        return pltpu.make_async_remote_copy(
            src_ref=final.at[head // sections, kind],
            dst_ref=out_columns(head, kind),
            send_sem=spread_send.at[head // sections, target, kind],
            recv_sem=spread_recv.at[head, kind],
            device_id={"section": target, "ctx": block},
            device_id_type=MESH,
        )

    def store_copy(head, kind):
        return pltpu.make_async_copy(
            final.at[head // sections, kind],
            out_columns(head, kind),
            store_sem.at[head // sections, kind],
        )

    @pl.when(section == 0)
    def _():
        for head in range(heads):
            for kind in range(2):
                load_shared(head, kind).start()

    @pl.when(cross)
    def _():
        for head in range(heads):
            for kind in range(2):
                load_group(head, kind).start()

    barrier = pltpu.get_barrier_semaphore()
    for step in range(1, sections):
        pl.semaphore_signal(
            barrier,
            inc=1,
            device_id={"section": lax.rem(section + step, sections), "ctx": block},
            device_id_type=MESH,
        )
    pl.semaphore_signal(
        barrier, inc=1, device_id={"section": section, "ctx": partner}, device_id_type=MESH
    )

    @pl.when(has_before)
    def _():
        pl.semaphore_signal(
            barrier,
            inc=1,
            device_id={"section": section, "ctx": block - REACH},
            device_id_type=MESH,
        )

    @pl.when(has_after)
    def _():
        pl.semaphore_signal(
            barrier,
            inc=1,
            device_id={"section": section, "ctx": block + REACH},
            device_id_type=MESH,
        )

    before_count = jnp.where(has_before, 1, 0)
    after_count = jnp.where(has_after, 1, 0)
    pl.semaphore_wait(barrier, sections + before_count + after_count)

    def finish(head):
        slot = head // sections
        for kind in range(2):

            @pl.when(cross)
            def _():
                final[slot, kind] = grads[head, kind, block_rows(REACH), :]

            @pl.when(section == 0)
            def _():
                final[slot, kind] = jnp.zeros((tokens, HEAD_SIZE), jnp.float32)

        for source in range(1, sections):

            @pl.when(section != source)
            def _():
                part_copy(head, source, section).wait_recv()
                final[slot] += part_in[slot, source].astype(jnp.float32)

        final[slot, 0] *= scale
        for kind in range(2):
            store_copy(head, kind).start()
            for step in range(1, sections):
                spread_copy(head, kind, lax.rem(section + step, sections)).start()

    @pl.when(section == 0)
    def _():
        for head in range(heads):
            for kind in range(2):
                load_shared(head, kind).wait()
                ring_copy(head, kind).start()

        @pl.loop(0, heads)
        def _(head):
            @pl.when(lax.rem(head, sections) == section)
            def _():
                finish(head)

    @pl.when(cross)
    def _():
        for index in range(tokens // ROWS):
            query_place = block * tokens + index * ROWS + lax.broadcasted_iota(
                jnp.int32, (8, ROWS), 1
            )
            start = jnp.zeros((8, ROWS), jnp.int32)
            end = 0
            for document in range(lengths_ref.shape[0]):
                end = end + lengths_ref[document]
                start = jnp.where(query_place >= end, end, start)
            key_place = (
                (block - REACH) * tokens
                + index * ROWS
                + lax.broadcasted_iota(jnp.int32, (span, ROWS), 0)
            )
            allowed = (key_place >= start[:1]) & (key_place <= query_place[:1])
            bias[index] = jnp.where(allowed, 0.0, MASKED_SCORE)

        @pl.when(block < REACH)
        def _():
            for head in range(heads):
                window[head, :, block_rows(0), :] = jnp.zeros((2, tokens, HEAD_SIZE), jnp.bfloat16)

        @pl.when(block == 0)
        def _():
            for head in range(heads):
                window[head, :, block_rows(1), :] = jnp.zeros((2, tokens, HEAD_SIZE), jnp.bfloat16)

        for head in range(heads):
            for kind in range(2):
                load_group(head, kind).wait()

        def pass_on(head):
            first = (2 * place) // (sections + 1)
            for kind in (first, 1 - first):
                ring_copy(head, kind).wait_recv()

                @pl.when(ring_goes_on(kind))
                def _():
                    ring_copy(head, kind).start()

            @pl.when(has_after)
            def _():
                hop_kv(head).start()

            @pl.when(odd == 0)
            def _():
                pair_kv(head, REACH).start()

        def pass_across(head):
            @pl.when(has_before & (odd == 1))
            def _():
                hop_kv(head).wait_recv()
                pair_kv(head, 0).start()

        def compute(head):
            for index in range(tokens // ROWS):
                rows = pl.ds(index * ROWS, ROWS)
                query = jnp.concatenate(
                    [
                        queries[head, rows, member * HEAD_SIZE : (member + 1) * HEAD_SIZE]
                        for member in range(QUERY_PER_KV)
                    ],
                    axis=0,
                )
                cotangent = jnp.concatenate(
                    [
                        cotangents[head, rows, member * HEAD_SIZE : (member + 1) * HEAD_SIZE]
                        for member in range(QUERY_PER_KV)
                    ],
                    axis=0,
                )
                chunks = span // ROWS
                top = jnp.full((8, QUERY_PER_KV * ROWS), -3e38, jnp.float32)
                for chunk in range(chunks):
                    keys = window[head, 0, pl.ds((index + chunk) * ROWS, ROWS), :]
                    mask = bias[index, pl.ds(chunk * ROWS, ROWS), :]
                    score = dot_last(keys, query) + jnp.concatenate([mask] * QUERY_PER_KV, axis=1)
                    score_buf[pl.ds(chunk * ROWS, ROWS), :] = score
                    top = jnp.maximum(top, folded(score, jnp.max))
                top = jnp.max(top, axis=0, keepdims=True)
                total = jnp.zeros((8, QUERY_PER_KV * ROWS), jnp.float32)
                delta = jnp.zeros((8, QUERY_PER_KV * ROWS), jnp.float32)
                for chunk in range(chunks):
                    here = pl.ds(chunk * ROWS, ROWS)
                    values = window[head, 1, pl.ds((index + chunk) * ROWS, ROWS), :]
                    power = jnp.exp2((score_buf[here, :] - top) * exponent_scale)
                    score_buf[here, :] = power
                    prob_grad = dot_last(values, cotangent)
                    prob_grad_buf[here, :] = prob_grad
                    total = total + folded(power, jnp.sum)
                    delta = delta + folded(power * prob_grad, jnp.sum)
                inverse = 1.0 / jnp.sum(total, axis=0, keepdims=True)
                delta = jnp.sum(delta, axis=0, keepdims=True) * inverse
                for chunk in range(chunks):
                    here = pl.ds(chunk * ROWS, ROWS)
                    there = pl.ds((index + chunk) * ROWS, ROWS)
                    prob = score_buf[here, :] * inverse
                    score_grad = prob * (prob_grad_buf[here, :] - delta)
                    key_grad = jnp.dot(
                        score_grad.astype(jnp.bfloat16), query, preferred_element_type=jnp.float32
                    )
                    value_grad = jnp.dot(
                        prob.astype(jnp.bfloat16), cotangent, preferred_element_type=jnp.float32
                    )
                    if index and chunk < chunks - 1:
                        key_grad = key_grad + grads[head, 0, there, :]
                        value_grad = value_grad + grads[head, 1, there, :]
                    grads[head, 0, there, :] = key_grad
                    grads[head, 1, there, :] = value_grad

        def attend(head):
            @pl.when(has_before & (odd == 0))
            def _():
                hop_kv(head).wait_recv()

            @pl.when(has_before | (odd == 1))
            def _():
                pair_kv(head, REACH).wait_recv()

            compute(head)

            @pl.when(has_before | (odd == 1))
            def _():
                pair_grads(head).start()

        def send_back(head):
            @pl.when(has_before)
            def _():
                @pl.when(odd == 0)
                def _():
                    hop_out[head] = grads[head, :, block_rows(0), :].astype(jnp.bfloat16)

                @pl.when(odd == 1)
                def _():
                    pair_grads(head).wait_recv()
                    hop_out[head] = (grads[head, :, block_rows(0), :] + pair_in[head]).astype(
                        jnp.bfloat16
                    )

                hop_grads(head).start()

        def gather(head):
            @pl.when(odd == 0)
            def _():
                pair_grads(head).wait_recv()
                grads[head, :, block_rows(REACH), :] += pair_in[head]

            @pl.when(has_after)
            def _():
                hop_grads(head).wait_recv()
                grads[head, :, block_rows(REACH), :] += hop_in[head].astype(jnp.float32)

            owner = lax.rem(head, sections)

            @pl.when(owner != section)
            def _():
                part_out[head] = grads[head, :, block_rows(REACH), :].astype(jnp.bfloat16)
                part_copy(head, section, owner).start()

        @pl.loop(0, heads + AHEAD + 3)
        def _(step):
            def stage(lag, run):
                head = step - lag

                @pl.when((head >= 0) & (head < heads))
                def _():
                    run(head)

            def finish_own(head):
                @pl.when(lax.rem(head, sections) == section)
                def _():
                    finish(head)

            stage(0, pass_on)
            stage(1, pass_across)
            stage(AHEAD + 1, send_back)
            stage(AHEAD + 2, gather)
            stage(AHEAD + 2, finish_own)
            stage(AHEAD, attend)

    @pl.loop(0, heads)
    def _(head):
        owner = lax.rem(head, sections)
        for kind in range(2):

            @pl.when(owner == section)
            def _():
                store_copy(head, kind).wait()
                for step in range(1, sections):
                    spread_copy(head, kind, lax.rem(section + step, sections)).wait_send()

            @pl.when(owner != section)
            def _():
                spread_copy(head, kind, owner).wait_recv()

            @pl.when(ring_goes_on(kind))
            def _():
                ring_copy(head, kind).wait_send()

        @pl.when(cross)
        def _():
            @pl.when(has_after)
            def _():
                hop_kv(head).wait_send()

            @pl.when(has_before | (odd == 0))
            def _():
                pair_kv(head, REACH).wait_send()

            @pl.when(has_before | (odd == 1))
            def _():
                pair_grads(head).wait_send()

            @pl.when(has_before)
            def _():
                hop_grads(head).wait_send()

            @pl.when(owner != section)
            def _():
                part_copy(head, section, owner).wait_send()


def on_device(projected, grad_out, doc_lengths):
    sections = lax.axis_size("section")
    blocks = lax.axis_size("ctx")
    tokens = projected.shape[1]
    heads = KV_HEAD_COUNT
    slots = -(-heads // sections)
    span = REACH * tokens + ROWS
    window_rows = (REACH + 1) * tokens
    group_width = QUERY_PER_KV * HEAD_SIZE
    bf16, f32 = jnp.bfloat16, jnp.float32
    dma = pltpu.SemaphoreType.DMA
    return pl.pallas_call(
        functools.partial(kernel, sections, blocks),
        out_shape=jax.ShapeDtypeStruct((tokens, 2 * heads * HEAD_SIZE), f32),
        in_specs=[
            pl.BlockSpec(memory_space=pltpu.SMEM),
            pl.BlockSpec(memory_space=pl.ANY),
            pl.BlockSpec(memory_space=pl.ANY),
        ],
        out_specs=pl.BlockSpec(memory_space=pl.ANY),
        scratch_shapes=[
            pltpu.VMEM((heads, tokens, group_width), bf16),
            pltpu.VMEM((heads, tokens, group_width), bf16),
            pltpu.VMEM((heads, 2, window_rows, HEAD_SIZE), bf16),
            pltpu.VMEM((tokens // ROWS, span, ROWS), f32),
            pltpu.VMEM((span, QUERY_PER_KV * ROWS), f32),
            pltpu.VMEM((span, QUERY_PER_KV * ROWS), f32),
            pltpu.VMEM((heads, 2, window_rows, HEAD_SIZE), f32),
            pltpu.VMEM((heads, 2, tokens, HEAD_SIZE), f32),
            pltpu.VMEM((heads, 2, tokens, HEAD_SIZE), bf16),
            pltpu.VMEM((heads, 2, tokens, HEAD_SIZE), bf16),
            pltpu.VMEM((heads, 2, tokens, HEAD_SIZE), bf16),
            pltpu.VMEM((slots, sections, 2, tokens, HEAD_SIZE), bf16),
            pltpu.VMEM((slots, 2, tokens, HEAD_SIZE), f32),
            dma((heads, 2)),
            dma((heads, 2)),
            dma((heads, 2)),
            dma((heads,)),
            dma((heads,)),
            dma((heads,)),
            dma((heads,)),
            dma((heads,)),
            dma((heads,)),
            dma((heads,)),
            dma((heads,)),
            dma((heads,)),
            dma((slots, sections)),
            dma((slots, sections, 2)),
            dma((heads, 2)),
            dma((slots, 2)),
        ],
        compiler_params=pltpu.CompilerParams(
            collective_id=0, has_side_effects=True, vmem_limit_bytes=56 * 1024 * 1024
        ),
        cost_estimate=pl.CostEstimate(
            flops=10 * heads * tokens * group_width * span // 1,
            bytes_accessed=16 * tokens * heads * group_width,
            transcendentals=heads * QUERY_PER_KV * tokens * span,
        ),
    )(doc_lengths, projected[0], grad_out[0])


def solution(mesh):
    return jax.shard_map(
        on_device,
        mesh=mesh,
        in_specs=(P("section", "ctx", None), P("section", "ctx", None), P()),
        out_specs=P("ctx", None),
        check_vma=False,
    )
```

```python
import functools
import math

import jax
import jax.numpy as jnp
from jax import lax
from jax.experimental import pallas as pl
from jax.experimental.pallas import tpu as pltpu
from jax.sharding import PartitionSpec as P

HEAD_SIZE = 128
KV_HEAD_COUNT = 8
QUERY_PER_KV = 3
REACH = 2
ROWS = 128
AHEAD = 3
MASKED_SCORE = -1e30
MESH = pl.DeviceIdType.MESH


def ring_swap(place, sections):
    half = sections // 2
    back = place // half
    return place * (1 - back) + back * (half + sections - 1 - place)


def dot_last(left, right):
    return lax.dot_general(
        left, right, (((1,), (1,)), ((), ())), preferred_element_type=jnp.float32
    )


def folded(value, reduce):
    return reduce(value.reshape(-1, 8, value.shape[-1]), axis=0)


def kernel(
    sections,
    blocks,
    lengths_ref,
    projected_ref,
    grad_out_ref,
    out_ref,
    queries,
    cotangents,
    window,
    bias,
    score_buf,
    prob_grad_buf,
    halves,
    grads,
    pair_in,
    hop_out,
    hop_in,
    part_out,
    part_in,
    final,
    load_sem,
    ring_send,
    ring_recv,
    hop_kv_send,
    hop_kv_recv,
    pair_kv_send,
    pair_kv_recv,
    pair_send,
    pair_recv,
    hop_send,
    hop_recv,
    part_send,
    part_recv,
    spread_send,
    spread_recv,
    store_sem,
):
    section = lax.axis_index("section")
    block = lax.axis_index("ctx")
    odd = lax.rem(block, 2)
    partner = block + 1 - 2 * odd
    place = ring_swap(section, sections)
    heads = KV_HEAD_COUNT
    tokens = out_ref.shape[0]
    width = heads * HEAD_SIZE
    group_width = QUERY_PER_KV * HEAD_SIZE
    span = REACH * tokens + ROWS
    scale = 1.0 / math.sqrt(HEAD_SIZE)
    exponent_scale = scale * math.log2(math.e)
    cross = section > 0
    has_before = block >= REACH
    has_after = block + REACH < blocks

    def block_rows(index):
        return pl.ds(index * tokens, tokens)

    def load_shared(head, kind):
        return pltpu.make_async_copy(
            projected_ref.at[:, pl.ds(kind * width + head * HEAD_SIZE, HEAD_SIZE)],
            window.at[head, kind, block_rows(REACH), :],
            load_sem.at[head, kind],
        )

    def load_group(head, kind):
        source, target = ((projected_ref, queries), (grad_out_ref, cotangents))[kind]
        return pltpu.make_async_copy(
            source.at[:, pl.ds(head * group_width, group_width)],
            target.at[head],
            load_sem.at[head, kind],
        )

    def ring_copy(head, kind):
        target_place = lax.rem(place + 1 - 2 * kind + sections, sections)
        own = window.at[head, kind, block_rows(REACH), :]
        return pltpu.make_async_remote_copy(
            src_ref=own,
            dst_ref=own,
            send_sem=ring_send.at[head, kind],
            recv_sem=ring_recv.at[head, kind],
            device_id={"section": ring_swap(target_place, sections), "ctx": block},
            device_id_type=MESH,
        )

    def ring_goes_on(kind):
        return lax.rem(place + 1 - 2 * kind + sections, sections) != 0

    def to_block(source, target, send_sem, recv_sem, target_block):
        return pltpu.make_async_remote_copy(
            src_ref=source,
            dst_ref=target,
            send_sem=send_sem,
            recv_sem=recv_sem,
            device_id={"section": section, "ctx": target_block},
            device_id_type=MESH,
        )

    def hop_kv(head):
        return to_block(
            window.at[head, :, block_rows(REACH), :],
            window.at[head, :, block_rows(0), :],
            hop_kv_send.at[head],
            hop_kv_recv.at[head],
            block + REACH,
        )

    def pair_kv(head, source_block):
        return to_block(
            window.at[head, :, block_rows(source_block), :],
            window.at[head, :, block_rows(1), :],
            pair_kv_send.at[head],
            pair_kv_recv.at[head],
            partner,
        )

    def pair_grads(head):
        return to_block(
            grads.at[head, :, block_rows(1), :],
            pair_in.at[head],
            pair_send.at[head],
            pair_recv.at[head],
            partner,
        )

    def hop_grads(head):
        return to_block(
            hop_out.at[head], hop_in.at[head], hop_send.at[head], hop_recv.at[head], block - REACH
        )

    def part_copy(head, source, target):
        return pltpu.make_async_remote_copy(
            src_ref=part_out.at[head],
            dst_ref=part_in.at[head // sections, source],
            send_sem=part_send.at[head],
            recv_sem=part_recv.at[head // sections, source],
            device_id={"section": target, "ctx": block},
            device_id_type=MESH,
        )

    def out_columns(head, kind):
        start = pl.multiple_of(kind * width + head * HEAD_SIZE, HEAD_SIZE)
        return out_ref.at[:, pl.ds(start, HEAD_SIZE)]

    def spread_copy(head, kind, target):
        return pltpu.make_async_remote_copy(
            src_ref=final.at[head // sections, kind],
            dst_ref=out_columns(head, kind),
            send_sem=spread_send.at[head // sections, target, kind],
            recv_sem=spread_recv.at[head, kind],
            device_id={"section": target, "ctx": block},
            device_id_type=MESH,
        )

    def store_copy(head, kind):
        return pltpu.make_async_copy(
            final.at[head // sections, kind],
            out_columns(head, kind),
            store_sem.at[head // sections, kind],
        )

    @pl.when(section == 0)
    def _():
        for head in range(heads):
            for kind in range(2):
                load_shared(head, kind).start()

    @pl.when(cross)
    def _():
        for head in range(heads):
            for kind in range(2):
                load_group(head, kind).start()

    barrier = pltpu.get_barrier_semaphore()
    for step in range(1, sections):
        pl.semaphore_signal(
            barrier,
            inc=1,
            device_id={"section": lax.rem(section + step, sections), "ctx": block},
            device_id_type=MESH,
        )
    pl.semaphore_signal(
        barrier, inc=1, device_id={"section": section, "ctx": partner}, device_id_type=MESH
    )

    @pl.when(has_before)
    def _():
        pl.semaphore_signal(
            barrier,
            inc=1,
            device_id={"section": section, "ctx": block - REACH},
            device_id_type=MESH,
        )

    @pl.when(has_after)
    def _():
        pl.semaphore_signal(
            barrier,
            inc=1,
            device_id={"section": section, "ctx": block + REACH},
            device_id_type=MESH,
        )

    before_count = jnp.where(has_before, 1, 0)
    after_count = jnp.where(has_after, 1, 0)
    pl.semaphore_wait(barrier, sections + before_count + after_count)

    def finish(head):
        slot = head // sections
        for kind in range(2):

            @pl.when(cross)
            def _():
                final[slot, kind] = grads[head, kind, block_rows(REACH), :]

            @pl.when(section == 0)
            def _():
                final[slot, kind] = jnp.zeros((tokens, HEAD_SIZE), jnp.float32)

        for source in range(1, sections):

            @pl.when(section != source)
            def _():
                part_copy(head, source, section).wait_recv()
                final[slot] += part_in[slot, source].astype(jnp.float32)

        final[slot, 0] *= scale
        for kind in range(2):
            store_copy(head, kind).start()
            for step in range(1, sections):
                spread_copy(head, kind, lax.rem(section + step, sections)).start()

    @pl.when(section == 0)
    def _():
        for head in range(heads):
            for kind in range(2):
                load_shared(head, kind).wait()
                ring_copy(head, kind).start()

        @pl.loop(0, heads)
        def _(head):
            @pl.when(lax.rem(head, sections) == section)
            def _():
                finish(head)

    @pl.when(cross)
    def _():
        for index in range(tokens // ROWS):
            query_place = block * tokens + index * ROWS + lax.broadcasted_iota(
                jnp.int32, (8, ROWS), 1
            )
            start = jnp.zeros((8, ROWS), jnp.int32)
            end = 0
            for document in range(lengths_ref.shape[0]):
                end = end + lengths_ref[document]
                start = jnp.where(query_place >= end, end, start)
            key_place = (
                (block - REACH) * tokens
                + index * ROWS
                + lax.broadcasted_iota(jnp.int32, (span, ROWS), 0)
            )
            allowed = (key_place >= start[:1]) & (key_place <= query_place[:1])
            bias[index] = jnp.where(allowed, 0.0, MASKED_SCORE)

        @pl.when(block < REACH)
        def _():
            for head in range(heads):
                window[head, :, block_rows(0), :] = jnp.zeros((2, tokens, HEAD_SIZE), jnp.bfloat16)

        @pl.when(block == 0)
        def _():
            for head in range(heads):
                window[head, :, block_rows(1), :] = jnp.zeros((2, tokens, HEAD_SIZE), jnp.bfloat16)

        for head in range(heads):
            for kind in range(2):
                load_group(head, kind).wait()

        def pass_on(head):
            first = (2 * place) // (sections + 1)
            for kind in (first, 1 - first):
                ring_copy(head, kind).wait_recv()

                @pl.when(ring_goes_on(kind))
                def _():
                    ring_copy(head, kind).start()

            @pl.when(has_after)
            def _():
                hop_kv(head).start()

            @pl.when(odd == 0)
            def _():
                pair_kv(head, REACH).start()

        def pass_across(head):
            @pl.when(has_before & (odd == 1))
            def _():
                hop_kv(head).wait_recv()
                pair_kv(head, 0).start()

        def compute(head):
            chunks = span // ROWS

            def stacked(array, index):
                rows = pl.ds(index * ROWS, ROWS)
                return jnp.concatenate(
                    [
                        array[head, rows, member * HEAD_SIZE : (member + 1) * HEAD_SIZE]
                        for member in range(QUERY_PER_KV)
                    ],
                    axis=0,
                )

            def products(index):
                band = pl.ds(index * ROWS, span)
                score_buf[index] = dot_last(window[head, 0, band, :], stacked(queries, index))
                prob_grad_buf[index] = dot_last(
                    window[head, 1, band, :], stacked(cotangents, index)
                )

            def soften(index):
                top = jnp.full((8, QUERY_PER_KV * ROWS), -3e38, jnp.float32)
                for chunk in range(chunks):
                    here = pl.ds(chunk * ROWS, ROWS)
                    mask = bias[index, here, :]
                    score = score_buf[index, here, :] + jnp.concatenate(
                        [mask] * QUERY_PER_KV, axis=1
                    )
                    score_buf[index, here, :] = score
                    top = jnp.maximum(top, folded(score, jnp.max))
                top = jnp.max(top, axis=0, keepdims=True)
                total = jnp.zeros((8, QUERY_PER_KV * ROWS), jnp.float32)
                delta = jnp.zeros((8, QUERY_PER_KV * ROWS), jnp.float32)
                for chunk in range(chunks):
                    here = pl.ds(chunk * ROWS, ROWS)
                    power = jnp.exp2((score_buf[index, here, :] - top) * exponent_scale)
                    score_buf[index, here, :] = power
                    total = total + folded(power, jnp.sum)
                    delta = delta + folded(power * prob_grad_buf[index, here, :], jnp.sum)
                inverse = 1.0 / jnp.sum(total, axis=0, keepdims=True)
                delta = jnp.sum(delta, axis=0, keepdims=True) * inverse
                for chunk in range(chunks):
                    here = pl.ds(chunk * ROWS, ROWS)
                    prob = score_buf[index, here, :] * inverse
                    score_grad = prob * (prob_grad_buf[index, here, :] - delta)
                    halves[index, 0, here, :] = score_grad.astype(jnp.bfloat16)
                    halves[index, 1, here, :] = prob.astype(jnp.bfloat16)

            def accumulate(index):
                for kind, array in enumerate((queries, cotangents)):
                    update = jnp.dot(
                        halves[index, kind],
                        stacked(array, index),
                        preferred_element_type=jnp.float32,
                    )
                    fresh = span - ROWS if index else 0
                    if index:
                        grads[head, kind, pl.ds(index * ROWS, fresh), :] += update[:fresh]
                    grads[head, kind, pl.ds(index * ROWS + fresh, span - fresh), :] = update[
                        fresh:
                    ]

            count = tokens // ROWS
            products(0)
            for index in range(count):
                if index + 1 < count:
                    products(index + 1)
                soften(index)
                accumulate(index)

        def attend(head):
            @pl.when(has_before & (odd == 0))
            def _():
                hop_kv(head).wait_recv()

            @pl.when(has_before | (odd == 1))
            def _():
                pair_kv(head, REACH).wait_recv()

            compute(head)

            @pl.when(has_before | (odd == 1))
            def _():
                pair_grads(head).start()

        def send_back(head):
            @pl.when(has_before)
            def _():
                @pl.when(odd == 0)
                def _():
                    hop_out[head] = grads[head, :, block_rows(0), :].astype(jnp.bfloat16)

                @pl.when(odd == 1)
                def _():
                    pair_grads(head).wait_recv()
                    hop_out[head] = (grads[head, :, block_rows(0), :] + pair_in[head]).astype(
                        jnp.bfloat16
                    )

                hop_grads(head).start()

        def gather(head):
            @pl.when(odd == 0)
            def _():
                pair_grads(head).wait_recv()
                grads[head, :, block_rows(REACH), :] += pair_in[head]

            @pl.when(has_after)
            def _():
                hop_grads(head).wait_recv()
                grads[head, :, block_rows(REACH), :] += hop_in[head].astype(jnp.float32)

            owner = lax.rem(head, sections)

            @pl.when(owner != section)
            def _():
                part_out[head] = grads[head, :, block_rows(REACH), :].astype(jnp.bfloat16)
                part_copy(head, section, owner).start()

        @pl.loop(0, heads + AHEAD + 3)
        def _(step):
            def stage(lag, run):
                head = step - lag

                @pl.when((head >= 0) & (head < heads))
                def _():
                    run(head)

            def finish_own(head):
                @pl.when(lax.rem(head, sections) == section)
                def _():
                    finish(head)

            stage(0, pass_on)
            stage(1, pass_across)
            stage(AHEAD + 1, send_back)
            stage(AHEAD + 2, gather)
            stage(AHEAD + 2, finish_own)
            stage(AHEAD, attend)

    @pl.loop(0, heads)
    def _(head):
        owner = lax.rem(head, sections)
        for kind in range(2):

            @pl.when(owner == section)
            def _():
                store_copy(head, kind).wait()
                for step in range(1, sections):
                    spread_copy(head, kind, lax.rem(section + step, sections)).wait_send()

            @pl.when(owner != section)
            def _():
                spread_copy(head, kind, owner).wait_recv()

            @pl.when(ring_goes_on(kind))
            def _():
                ring_copy(head, kind).wait_send()

        @pl.when(cross)
        def _():
            @pl.when(has_after)
            def _():
                hop_kv(head).wait_send()

            @pl.when(has_before | (odd == 0))
            def _():
                pair_kv(head, REACH).wait_send()

            @pl.when(has_before | (odd == 1))
            def _():
                pair_grads(head).wait_send()

            @pl.when(has_before)
            def _():
                hop_grads(head).wait_send()

            @pl.when(owner != section)
            def _():
                part_copy(head, section, owner).wait_send()


def on_device(projected, grad_out, doc_lengths):
    sections = lax.axis_size("section")
    blocks = lax.axis_size("ctx")
    tokens = projected.shape[1]
    heads = KV_HEAD_COUNT
    slots = -(-heads // sections)
    span = REACH * tokens + ROWS
    window_rows = (REACH + 1) * tokens
    group_width = QUERY_PER_KV * HEAD_SIZE
    bf16, f32 = jnp.bfloat16, jnp.float32
    dma = pltpu.SemaphoreType.DMA
    return pl.pallas_call(
        functools.partial(kernel, sections, blocks),
        out_shape=jax.ShapeDtypeStruct((tokens, 2 * heads * HEAD_SIZE), f32),
        in_specs=[
            pl.BlockSpec(memory_space=pltpu.SMEM),
            pl.BlockSpec(memory_space=pl.ANY),
            pl.BlockSpec(memory_space=pl.ANY),
        ],
        out_specs=pl.BlockSpec(memory_space=pl.ANY),
        scratch_shapes=[
            pltpu.VMEM((heads, tokens, group_width), bf16),
            pltpu.VMEM((heads, tokens, group_width), bf16),
            pltpu.VMEM((heads, 2, window_rows, HEAD_SIZE), bf16),
            pltpu.VMEM((tokens // ROWS, span, ROWS), f32),
            pltpu.VMEM((tokens // ROWS, span, QUERY_PER_KV * ROWS), f32),
            pltpu.VMEM((tokens // ROWS, span, QUERY_PER_KV * ROWS), f32),
            pltpu.VMEM((tokens // ROWS, 2, span, QUERY_PER_KV * ROWS), bf16),
            pltpu.VMEM((heads, 2, window_rows, HEAD_SIZE), f32),
            pltpu.VMEM((heads, 2, tokens, HEAD_SIZE), f32),
            pltpu.VMEM((heads, 2, tokens, HEAD_SIZE), bf16),
            pltpu.VMEM((heads, 2, tokens, HEAD_SIZE), bf16),
            pltpu.VMEM((heads, 2, tokens, HEAD_SIZE), bf16),
            pltpu.VMEM((slots, sections, 2, tokens, HEAD_SIZE), bf16),
            pltpu.VMEM((slots, 2, tokens, HEAD_SIZE), f32),
            dma((heads, 2)),
            dma((heads, 2)),
            dma((heads, 2)),
            dma((heads,)),
            dma((heads,)),
            dma((heads,)),
            dma((heads,)),
            dma((heads,)),
            dma((heads,)),
            dma((heads,)),
            dma((heads,)),
            dma((heads,)),
            dma((slots, sections)),
            dma((slots, sections, 2)),
            dma((heads, 2)),
            dma((slots, 2)),
        ],
        compiler_params=pltpu.CompilerParams(
            collective_id=0, has_side_effects=True, vmem_limit_bytes=56 * 1024 * 1024
        ),
        cost_estimate=pl.CostEstimate(
            flops=10 * heads * tokens * group_width * span // 1,
            bytes_accessed=16 * tokens * heads * group_width,
            transcendentals=heads * QUERY_PER_KV * tokens * span,
        ),
    )(doc_lengths, projected[0], grad_out[0])


def solution(mesh):
    return jax.shard_map(
        on_device,
        mesh=mesh,
        in_specs=(P("section", "ctx", None), P("section", "ctx", None), P()),
        out_specs=P("ctx", None),
        check_vma=False,
    )
```

```python
import functools
import math

import jax
import jax.numpy as jnp
from jax import lax
from jax.experimental import pallas as pl
from jax.experimental.pallas import tpu as pltpu
from jax.sharding import PartitionSpec as P

HEAD_SIZE = 128
KV_HEAD_COUNT = 8
QUERY_PER_KV = 3
REACH = 2
ROWS = 128
AHEAD = 3
MASKED_SCORE = -1e30
MESH = pl.DeviceIdType.MESH


def ring_swap(place, sections):
    half = sections // 2
    back = place // half
    return place * (1 - back) + back * (half + sections - 1 - place)


def dot_last(left, right):
    return lax.dot_general(
        left, right, (((1,), (1,)), ((), ())), preferred_element_type=jnp.float32
    )


def folded(value, reduce):
    return reduce(value.reshape(-1, 8, value.shape[-1]), axis=0)


def kernel(
    sections,
    blocks,
    lengths_ref,
    projected_ref,
    grad_out_ref,
    out_ref,
    queries,
    cotangents,
    window,
    bias,
    score_buf,
    prob_grad_buf,
    halves,
    grads,
    pair_in,
    hop_out,
    hop_in,
    part_out,
    part_in,
    final,
    final_half,
    load_sem,
    ring_send,
    ring_recv,
    hop_kv_send,
    hop_kv_recv,
    pair_kv_send,
    pair_kv_recv,
    pair_send,
    pair_recv,
    hop_send,
    hop_recv,
    part_send,
    part_recv,
    spread_send,
    spread_recv,
    store_sem,
):
    section = lax.axis_index("section")
    block = lax.axis_index("ctx")
    odd = lax.rem(block, 2)
    partner = block + 1 - 2 * odd
    place = ring_swap(section, sections)
    heads = KV_HEAD_COUNT
    tokens = out_ref.shape[0]
    width = heads * HEAD_SIZE
    group_width = QUERY_PER_KV * HEAD_SIZE
    span = REACH * tokens + ROWS
    scale = 1.0 / math.sqrt(HEAD_SIZE)
    exponent_scale = scale * math.log2(math.e)
    cross = section > 0
    has_before = block >= REACH
    has_after = block + REACH < blocks

    def block_rows(index):
        return pl.ds(index * tokens, tokens)

    def load_shared(head, kind):
        return pltpu.make_async_copy(
            projected_ref.at[:, pl.ds(kind * width + head * HEAD_SIZE, HEAD_SIZE)],
            window.at[head, kind, block_rows(REACH), :],
            load_sem.at[head, kind],
        )

    def load_group(head, kind):
        source, target = ((projected_ref, queries), (grad_out_ref, cotangents))[kind]
        return pltpu.make_async_copy(
            source.at[:, pl.ds(head * group_width, group_width)],
            target.at[head],
            load_sem.at[head, kind],
        )

    def ring_copy(head, kind, way):
        target_place = lax.rem(place + 1 - 2 * way + sections, sections)
        own = window.at[head, kind, block_rows(REACH), :]
        return pltpu.make_async_remote_copy(
            src_ref=own,
            dst_ref=own,
            send_sem=ring_send.at[head, kind, way],
            recv_sem=ring_recv.at[head, kind],
            device_id={"section": ring_swap(target_place, sections), "ctx": block},
            device_id_type=MESH,
        )

    def ring_sends(kind, way):
        middle = sections // 2
        if way == 0:
            return place < middle if kind == 0 else place + 1 < middle
        above = lax.rem(place - 1 + sections, sections)
        starts = (place == 0) | (place > middle)
        return starts & (above > middle if kind == 0 else above >= middle)

    def ring_start(head, kind):
        for way in range(2):

            @pl.when(ring_sends(kind, way))
            def _():
                ring_copy(head, kind, way).start()

    def to_block(source, target, send_sem, recv_sem, target_block):
        return pltpu.make_async_remote_copy(
            src_ref=source,
            dst_ref=target,
            send_sem=send_sem,
            recv_sem=recv_sem,
            device_id={"section": section, "ctx": target_block},
            device_id_type=MESH,
        )

    def hop_kv(head):
        return to_block(
            window.at[head, :, block_rows(REACH), :],
            window.at[head, :, block_rows(0), :],
            hop_kv_send.at[head],
            hop_kv_recv.at[head],
            block + REACH,
        )

    def pair_kv(head, source_block):
        return to_block(
            window.at[head, :, block_rows(source_block), :],
            window.at[head, :, block_rows(1), :],
            pair_kv_send.at[head],
            pair_kv_recv.at[head],
            partner,
        )

    def pair_grads(head):
        return to_block(
            grads.at[head, :, block_rows(1), :],
            pair_in.at[head],
            pair_send.at[head],
            pair_recv.at[head],
            partner,
        )

    def hop_grads(head):
        return to_block(
            hop_out.at[head], hop_in.at[head], hop_send.at[head], hop_recv.at[head], block - REACH
        )

    def part_copy(head, source, target):
        return pltpu.make_async_remote_copy(
            src_ref=part_out.at[head],
            dst_ref=part_in.at[head // sections, source],
            send_sem=part_send.at[head],
            recv_sem=part_recv.at[head // sections, source],
            device_id={"section": target, "ctx": block},
            device_id_type=MESH,
        )

    def out_columns(head, kind):
        start = pl.multiple_of(kind * width + head * HEAD_SIZE, HEAD_SIZE)
        return out_ref.at[:, pl.ds(start, HEAD_SIZE)]

    def spread_copy(head, kind, target):
        return pltpu.make_async_remote_copy(
            src_ref=final_half.at[head // sections, kind],
            dst_ref=out_columns(head, kind),
            send_sem=spread_send.at[head // sections, target, kind],
            recv_sem=spread_recv.at[head, kind],
            device_id={"section": target, "ctx": block},
            device_id_type=MESH,
        )

    def store_copy(head, kind):
        return pltpu.make_async_copy(
            final_half.at[head // sections, kind],
            out_columns(head, kind),
            store_sem.at[head // sections, kind],
        )

    @pl.when(section == 0)
    def _():
        for head in range(heads):
            for kind in range(2):
                load_shared(head, kind).start()

    @pl.when(cross)
    def _():
        for head in range(heads):
            for kind in range(2):
                load_group(head, kind).start()

    barrier = pltpu.get_barrier_semaphore()
    for step in range(1, sections):
        pl.semaphore_signal(
            barrier,
            inc=1,
            device_id={"section": lax.rem(section + step, sections), "ctx": block},
            device_id_type=MESH,
        )
    pl.semaphore_signal(
        barrier, inc=1, device_id={"section": section, "ctx": partner}, device_id_type=MESH
    )

    @pl.when(has_before)
    def _():
        pl.semaphore_signal(
            barrier,
            inc=1,
            device_id={"section": section, "ctx": block - REACH},
            device_id_type=MESH,
        )

    @pl.when(has_after)
    def _():
        pl.semaphore_signal(
            barrier,
            inc=1,
            device_id={"section": section, "ctx": block + REACH},
            device_id_type=MESH,
        )

    before_count = jnp.where(has_before, 1, 0)
    after_count = jnp.where(has_after, 1, 0)
    pl.semaphore_wait(barrier, sections + before_count + after_count)

    def finish(head):
        slot = head // sections
        for kind in range(2):

            @pl.when(cross)
            def _():
                final[slot, kind] = grads[head, kind, block_rows(REACH), :]

            @pl.when(section == 0)
            def _():
                final[slot, kind] = jnp.zeros((tokens, HEAD_SIZE), jnp.float32)

        for source in range(1, sections):

            @pl.when(section != source)
            def _():
                part_copy(head, source, section).wait_recv()
                final[slot] += part_in[slot, source].astype(jnp.float32)

        final_half[slot, 0] = (final[slot, 0] * scale).astype(jnp.bfloat16)
        final_half[slot, 1] = final[slot, 1].astype(jnp.bfloat16)
        for kind in range(2):
            store_copy(head, kind).start()
            for step in range(1, sections):
                spread_copy(head, kind, lax.rem(section + step, sections)).start()

    @pl.when(section == 0)
    def _():
        for head in range(heads):
            for kind in range(2):
                load_shared(head, kind).wait()
                ring_start(head, kind)

        @pl.loop(0, heads)
        def _(head):
            @pl.when(lax.rem(head, sections) == section)
            def _():
                finish(head)

    @pl.when(cross)
    def _():
        for index in range(tokens // ROWS):
            query_place = block * tokens + index * ROWS + lax.broadcasted_iota(
                jnp.int32, (8, ROWS), 1
            )
            start = jnp.zeros((8, ROWS), jnp.int32)
            end = 0
            for document in range(lengths_ref.shape[0]):
                end = end + lengths_ref[document]
                start = jnp.where(query_place >= end, end, start)
            key_place = (
                (block - REACH) * tokens
                + index * ROWS
                + lax.broadcasted_iota(jnp.int32, (span, ROWS), 0)
            )
            allowed = (key_place >= start[:1]) & (key_place <= query_place[:1])
            bias[index] = jnp.where(allowed, 0.0, MASKED_SCORE)

        @pl.when(block < REACH)
        def _():
            for head in range(heads):
                window[head, :, block_rows(0), :] = jnp.zeros((2, tokens, HEAD_SIZE), jnp.bfloat16)

        @pl.when(block == 0)
        def _():
            for head in range(heads):
                window[head, :, block_rows(1), :] = jnp.zeros((2, tokens, HEAD_SIZE), jnp.bfloat16)

        for head in range(heads):
            for kind in range(2):
                load_group(head, kind).wait()

        def pass_on(head):
            for kind in range(2):
                ring_copy(head, kind, 0).wait_recv()
                ring_start(head, kind)

            @pl.when(has_after)
            def _():
                hop_kv(head).start()

            @pl.when(odd == 0)
            def _():
                pair_kv(head, REACH).start()

        def pass_across(head):
            @pl.when(has_before & (odd == 1))
            def _():
                hop_kv(head).wait_recv()
                pair_kv(head, 0).start()

        def compute(head):
            chunks = span // ROWS

            def stacked(array, index):
                rows = pl.ds(index * ROWS, ROWS)
                return jnp.concatenate(
                    [
                        array[head, rows, member * HEAD_SIZE : (member + 1) * HEAD_SIZE]
                        for member in range(QUERY_PER_KV)
                    ],
                    axis=0,
                )

            def products(index):
                band = pl.ds(index * ROWS, span)
                score_buf[index] = dot_last(window[head, 0, band, :], stacked(queries, index))
                prob_grad_buf[index] = dot_last(
                    window[head, 1, band, :], stacked(cotangents, index)
                )

            def soften(index):
                top = jnp.full((8, QUERY_PER_KV * ROWS), -3e38, jnp.float32)
                for chunk in range(chunks):
                    here = pl.ds(chunk * ROWS, ROWS)
                    mask = bias[index, here, :]
                    score = score_buf[index, here, :] + jnp.concatenate(
                        [mask] * QUERY_PER_KV, axis=1
                    )
                    score_buf[index, here, :] = score
                    top = jnp.maximum(top, folded(score, jnp.max))
                top = jnp.max(top, axis=0, keepdims=True)
                total = jnp.zeros((8, QUERY_PER_KV * ROWS), jnp.float32)
                delta = jnp.zeros((8, QUERY_PER_KV * ROWS), jnp.float32)
                for chunk in range(chunks):
                    here = pl.ds(chunk * ROWS, ROWS)
                    power = jnp.exp2((score_buf[index, here, :] - top) * exponent_scale)
                    score_buf[index, here, :] = power
                    total = total + folded(power, jnp.sum)
                    delta = delta + folded(power * prob_grad_buf[index, here, :], jnp.sum)
                inverse = 1.0 / jnp.sum(total, axis=0, keepdims=True)
                delta = jnp.sum(delta, axis=0, keepdims=True) * inverse
                for chunk in range(chunks):
                    here = pl.ds(chunk * ROWS, ROWS)
                    prob = score_buf[index, here, :] * inverse
                    score_grad = prob * (prob_grad_buf[index, here, :] - delta)
                    halves[index, 0, here, :] = score_grad.astype(jnp.bfloat16)
                    halves[index, 1, here, :] = prob.astype(jnp.bfloat16)

            def accumulate(index):
                for kind, array in enumerate((queries, cotangents)):
                    update = jnp.dot(
                        halves[index, kind],
                        stacked(array, index),
                        preferred_element_type=jnp.float32,
                    )
                    fresh = span - ROWS if index else 0
                    if index:
                        grads[head, kind, pl.ds(index * ROWS, fresh), :] += update[:fresh]
                    grads[head, kind, pl.ds(index * ROWS + fresh, span - fresh), :] = update[
                        fresh:
                    ]

            count = tokens // ROWS
            products(0)
            for index in range(count):
                if index + 1 < count:
                    products(index + 1)
                soften(index)
                accumulate(index)

        def attend(head):
            @pl.when(has_before & (odd == 0))
            def _():
                hop_kv(head).wait_recv()

            @pl.when(has_before | (odd == 1))
            def _():
                pair_kv(head, REACH).wait_recv()

            compute(head)

            @pl.when(has_before | (odd == 1))
            def _():
                pair_grads(head).start()

        def send_back(head):
            @pl.when(has_before)
            def _():
                @pl.when(odd == 0)
                def _():
                    hop_out[head] = grads[head, :, block_rows(0), :].astype(jnp.bfloat16)

                @pl.when(odd == 1)
                def _():
                    pair_grads(head).wait_recv()
                    hop_out[head] = (grads[head, :, block_rows(0), :] + pair_in[head]).astype(
                        jnp.bfloat16
                    )

                hop_grads(head).start()

        def gather(head):
            @pl.when(odd == 0)
            def _():
                pair_grads(head).wait_recv()
                grads[head, :, block_rows(REACH), :] += pair_in[head]

            @pl.when(has_after)
            def _():
                hop_grads(head).wait_recv()
                grads[head, :, block_rows(REACH), :] += hop_in[head].astype(jnp.float32)

            owner = lax.rem(head, sections)

            @pl.when(owner != section)
            def _():
                part_out[head] = grads[head, :, block_rows(REACH), :].astype(jnp.bfloat16)
                part_copy(head, section, owner).start()

        @pl.loop(0, heads + AHEAD + 4)
        def _(step):
            def stage(lag, run):
                head = step - lag

                @pl.when((head >= 0) & (head < heads))
                def _():
                    run(head)

            def finish_own(head):
                @pl.when(lax.rem(head, sections) == section)
                def _():
                    finish(head)

            stage(0, pass_on)
            stage(1, pass_across)
            stage(AHEAD, attend)
            stage(AHEAD + 1, send_back)
            stage(AHEAD + 2, gather)
            stage(AHEAD + 3, finish_own)

    @pl.loop(0, heads)
    def _(head):
        owner = lax.rem(head, sections)
        for kind in range(2):

            @pl.when(owner == section)
            def _():
                store_copy(head, kind).wait()
                for step in range(1, sections):
                    spread_copy(head, kind, lax.rem(section + step, sections)).wait_send()

            @pl.when(owner != section)
            def _():
                spread_copy(head, kind, owner).wait_recv()

            for way in range(2):

                @pl.when(ring_sends(kind, way))
                def _():
                    ring_copy(head, kind, way).wait_send()

        @pl.when(cross)
        def _():
            @pl.when(has_after)
            def _():
                hop_kv(head).wait_send()

            @pl.when(has_before | (odd == 0))
            def _():
                pair_kv(head, REACH).wait_send()

            @pl.when(has_before | (odd == 1))
            def _():
                pair_grads(head).wait_send()

            @pl.when(has_before)
            def _():
                hop_grads(head).wait_send()

            @pl.when(owner != section)
            def _():
                part_copy(head, section, owner).wait_send()


def on_device(projected, grad_out, doc_lengths):
    sections = lax.axis_size("section")
    blocks = lax.axis_size("ctx")
    tokens = projected.shape[1]
    heads = KV_HEAD_COUNT
    slots = -(-heads // sections)
    span = REACH * tokens + ROWS
    window_rows = (REACH + 1) * tokens
    group_width = QUERY_PER_KV * HEAD_SIZE
    bf16, f32 = jnp.bfloat16, jnp.float32
    dma = pltpu.SemaphoreType.DMA
    return pl.pallas_call(
        functools.partial(kernel, sections, blocks),
        out_shape=jax.ShapeDtypeStruct((tokens, 2 * heads * HEAD_SIZE), bf16),
        in_specs=[
            pl.BlockSpec(memory_space=pltpu.SMEM),
            pl.BlockSpec(memory_space=pl.ANY),
            pl.BlockSpec(memory_space=pl.ANY),
        ],
        out_specs=pl.BlockSpec(memory_space=pl.ANY),
        scratch_shapes=[
            pltpu.VMEM((heads, tokens, group_width), bf16),
            pltpu.VMEM((heads, tokens, group_width), bf16),
            pltpu.VMEM((heads, 2, window_rows, HEAD_SIZE), bf16),
            pltpu.VMEM((tokens // ROWS, span, ROWS), f32),
            pltpu.VMEM((tokens // ROWS, span, QUERY_PER_KV * ROWS), f32),
            pltpu.VMEM((tokens // ROWS, span, QUERY_PER_KV * ROWS), f32),
            pltpu.VMEM((tokens // ROWS, 2, span, QUERY_PER_KV * ROWS), bf16),
            pltpu.VMEM((heads, 2, window_rows, HEAD_SIZE), f32),
            pltpu.VMEM((heads, 2, tokens, HEAD_SIZE), f32),
            pltpu.VMEM((heads, 2, tokens, HEAD_SIZE), bf16),
            pltpu.VMEM((heads, 2, tokens, HEAD_SIZE), bf16),
            pltpu.VMEM((heads, 2, tokens, HEAD_SIZE), bf16),
            pltpu.VMEM((slots, sections, 2, tokens, HEAD_SIZE), bf16),
            pltpu.VMEM((slots, 2, tokens, HEAD_SIZE), f32),
            pltpu.VMEM((slots, 2, tokens, HEAD_SIZE), bf16),
            dma((heads, 2)),
            dma((heads, 2, 2)),
            dma((heads, 2)),
            dma((heads,)),
            dma((heads,)),
            dma((heads,)),
            dma((heads,)),
            dma((heads,)),
            dma((heads,)),
            dma((heads,)),
            dma((heads,)),
            dma((heads,)),
            dma((slots, sections)),
            dma((slots, sections, 2)),
            dma((heads, 2)),
            dma((slots, 2)),
        ],
        compiler_params=pltpu.CompilerParams(
            collective_id=0, has_side_effects=True, vmem_limit_bytes=56 * 1024 * 1024
        ),
        cost_estimate=pl.CostEstimate(
            flops=10 * heads * tokens * group_width * span // 1,
            bytes_accessed=16 * tokens * heads * group_width,
            transcendentals=heads * QUERY_PER_KV * tokens * span,
        ),
    )(doc_lengths, projected[0], grad_out[0]).astype(f32)


def solution(mesh):
    return jax.shard_map(
        on_device,
        mesh=mesh,
        in_specs=(P("section", "ctx", None), P("section", "ctx", None), P()),
        out_specs=P("ctx", None),
        check_vma=False,
    )
```

```python
import functools
import math

import jax
import jax.numpy as jnp
from jax import lax
from jax.experimental import pallas as pl
from jax.experimental.pallas import tpu as pltpu
from jax.sharding import PartitionSpec as P

HEAD_SIZE = 128
KV_HEAD_COUNT = 8
QUERY_PER_KV = 3
REACH = 2
ROWS = 128
AHEAD = 2
MASKED_SCORE = -1e30
MESH = pl.DeviceIdType.MESH


def ring_swap(place, sections):
    half = sections // 2
    back = place // half
    return place * (1 - back) + back * (half + sections - 1 - place)


def dot_last(left, right):
    return lax.dot_general(
        left, right, (((1,), (1,)), ((), ())), preferred_element_type=jnp.float32
    )


def folded(value, reduce):
    return reduce(value.reshape(-1, 8, value.shape[-1]), axis=0)


def kernel(
    sections,
    blocks,
    lengths_ref,
    projected_ref,
    grad_out_ref,
    out_ref,
    queries,
    cotangents,
    window,
    bias,
    score_buf,
    prob_grad_buf,
    halves,
    grads,
    pair_in,
    hop_out,
    hop_in,
    part_out,
    part_in,
    final,
    final_half,
    load_sem,
    ring_send,
    ring_recv,
    hop_kv_send,
    hop_kv_recv,
    pair_kv_send,
    pair_kv_recv,
    pair_send,
    pair_recv,
    hop_send,
    hop_recv,
    part_send,
    part_recv,
    spread_send,
    spread_recv,
    store_sem,
):
    section = lax.axis_index("section")
    block = lax.axis_index("ctx")
    odd = lax.rem(block, 2)
    partner = block + 1 - 2 * odd
    place = ring_swap(section, sections)
    heads = KV_HEAD_COUNT
    tokens = out_ref.shape[0]
    width = heads * HEAD_SIZE
    group_width = QUERY_PER_KV * HEAD_SIZE
    span = REACH * tokens + ROWS
    scale = 1.0 / math.sqrt(HEAD_SIZE)
    exponent_scale = scale * math.log2(math.e)
    cross = section > 0
    has_before = block >= REACH
    has_after = block + REACH < blocks

    def block_rows(index):
        return pl.ds(index * tokens, tokens)

    def load_shared(head, kind):
        return pltpu.make_async_copy(
            projected_ref.at[:, pl.ds(kind * width + head * HEAD_SIZE, HEAD_SIZE)],
            window.at[head, kind, block_rows(REACH), :],
            load_sem.at[head, kind],
        )

    def load_group(head, kind):
        source, target = ((projected_ref, queries), (grad_out_ref, cotangents))[kind]
        return pltpu.make_async_copy(
            source.at[:, pl.ds(head * group_width, group_width)],
            target.at[head],
            load_sem.at[head, kind],
        )

    def ring_copy(head, kind, way):
        target_place = lax.rem(place + 1 - 2 * way + sections, sections)
        own = window.at[head, kind, block_rows(REACH), :]
        return pltpu.make_async_remote_copy(
            src_ref=own,
            dst_ref=own,
            send_sem=ring_send.at[head, kind, way],
            recv_sem=ring_recv.at[head, kind],
            device_id={"section": ring_swap(target_place, sections), "ctx": block},
            device_id_type=MESH,
        )

    def ring_sends(kind, way):
        middle = sections // 2
        if way == 0:
            return place < middle if kind == 0 else place + 1 < middle
        above = lax.rem(place - 1 + sections, sections)
        starts = (place == 0) | (place > middle)
        return starts & (above > middle if kind == 0 else above >= middle)

    def ring_start(head, kind):
        for way in range(2):

            @pl.when(ring_sends(kind, way))
            def _():
                ring_copy(head, kind, way).start()

    def ring_sent(head):
        for kind in range(2):
            for way in range(2):

                @pl.when(ring_sends(kind, way))
                def _():
                    ring_copy(head, kind, way).wait_send()

    def to_block(source, target, send_sem, recv_sem, target_block):
        return pltpu.make_async_remote_copy(
            src_ref=source,
            dst_ref=target,
            send_sem=send_sem,
            recv_sem=recv_sem,
            device_id={"section": section, "ctx": target_block},
            device_id_type=MESH,
        )

    def hop_kv(head):
        return to_block(
            window.at[head, :, block_rows(REACH), :],
            window.at[head, :, block_rows(0), :],
            hop_kv_send.at[head],
            hop_kv_recv.at[head],
            block + REACH,
        )

    def pair_kv(head, source_block):
        return to_block(
            window.at[head, :, block_rows(source_block), :],
            window.at[head, :, block_rows(1), :],
            pair_kv_send.at[head],
            pair_kv_recv.at[head],
            partner,
        )

    def pair_grads(head):
        return to_block(
            grads.at[head, :, block_rows(1), :],
            pair_in.at[head],
            pair_send.at[head],
            pair_recv.at[head],
            partner,
        )

    def hop_grads(head):
        return to_block(
            hop_out.at[head], hop_in.at[head], hop_send.at[head], hop_recv.at[head], block - REACH
        )

    def part_copy(head, source, target):
        return pltpu.make_async_remote_copy(
            src_ref=part_out.at[head],
            dst_ref=part_in.at[head // sections, source],
            send_sem=part_send.at[head],
            recv_sem=part_recv.at[head // sections, source],
            device_id={"section": target, "ctx": block},
            device_id_type=MESH,
        )

    def out_columns(head, kind):
        start = pl.multiple_of(kind * width + head * HEAD_SIZE, HEAD_SIZE)
        return out_ref.at[:, pl.ds(start, HEAD_SIZE)]

    def spread_copy(head, kind, target):
        return pltpu.make_async_remote_copy(
            src_ref=final_half.at[head // sections, kind],
            dst_ref=out_columns(head, kind),
            send_sem=spread_send.at[head // sections, target, kind],
            recv_sem=spread_recv.at[head, kind],
            device_id={"section": target, "ctx": block},
            device_id_type=MESH,
        )

    def store_copy(head, kind):
        return pltpu.make_async_copy(
            final_half.at[head // sections, kind],
            out_columns(head, kind),
            store_sem.at[head // sections, kind],
        )

    @pl.when(section == 0)
    def _():
        for head in range(heads):
            for kind in range(2):
                load_shared(head, kind).start()

    @pl.when(cross)
    def _():
        for head in range(heads):
            for kind in range(2):
                load_group(head, kind).start()

    barrier = pltpu.get_barrier_semaphore()
    for step in range(1, sections):
        pl.semaphore_signal(
            barrier,
            inc=1,
            device_id={"section": lax.rem(section + step, sections), "ctx": block},
            device_id_type=MESH,
        )
    pl.semaphore_signal(
        barrier, inc=1, device_id={"section": section, "ctx": partner}, device_id_type=MESH
    )

    @pl.when(has_before)
    def _():
        pl.semaphore_signal(
            barrier,
            inc=1,
            device_id={"section": section, "ctx": block - REACH},
            device_id_type=MESH,
        )

    @pl.when(has_after)
    def _():
        pl.semaphore_signal(
            barrier,
            inc=1,
            device_id={"section": section, "ctx": block + REACH},
            device_id_type=MESH,
        )

    before_count = jnp.where(has_before, 1, 0)
    after_count = jnp.where(has_after, 1, 0)
    pl.semaphore_wait(barrier, sections + before_count + after_count)

    def finish(head):
        slot = head // sections
        for kind in range(2):

            @pl.when(cross)
            def _():
                final[slot, kind] = grads[head, kind, block_rows(REACH), :]

            @pl.when(section == 0)
            def _():
                final[slot, kind] = jnp.zeros((tokens, HEAD_SIZE), jnp.float32)

        for source in range(1, sections):

            @pl.when(section != source)
            def _():
                part_copy(head, source, section).wait_recv()
                final[slot] += part_in[slot, source].astype(jnp.float32)

        final_half[slot, 0] = (final[slot, 0] * scale).astype(jnp.bfloat16)
        final_half[slot, 1] = final[slot, 1].astype(jnp.bfloat16)
        for kind in range(2):
            store_copy(head, kind).start()
            for step in range(1, sections):
                spread_copy(head, kind, lax.rem(section + step, sections)).start()

    @pl.when(section == 0)
    def _():
        for head in range(heads):
            for kind in range(2):
                load_shared(head, kind).wait()
                ring_start(head, kind)
            if head >= 2:
                ring_sent(head - 2)
        for head in range(heads - 2, heads):
            ring_sent(head)

        @pl.loop(0, heads)
        def _(head):
            @pl.when(lax.rem(head, sections) == section)
            def _():
                finish(head)

    @pl.when(cross)
    def _():
        for index in range(tokens // ROWS):
            query_place = block * tokens + index * ROWS + lax.broadcasted_iota(
                jnp.int32, (8, ROWS), 1
            )
            start = jnp.zeros((8, ROWS), jnp.int32)
            end = 0
            for document in range(lengths_ref.shape[0]):
                end = end + lengths_ref[document]
                start = jnp.where(query_place >= end, end, start)
            key_place = (
                (block - REACH) * tokens
                + index * ROWS
                + lax.broadcasted_iota(jnp.int32, (span, ROWS), 0)
            )
            allowed = (key_place >= start[:1]) & (key_place <= query_place[:1])
            bias[index] = jnp.where(allowed, 0.0, MASKED_SCORE)

        @pl.when(block < REACH)
        def _():
            for head in range(heads):
                window[head, :, block_rows(0), :] = jnp.zeros((2, tokens, HEAD_SIZE), jnp.bfloat16)

        @pl.when(block == 0)
        def _():
            for head in range(heads):
                window[head, :, block_rows(1), :] = jnp.zeros((2, tokens, HEAD_SIZE), jnp.bfloat16)

        for head in range(heads):
            for kind in range(2):
                load_group(head, kind).wait()

        def pass_on(head):
            for kind in range(2):
                ring_copy(head, kind, 0).wait_recv()
                ring_start(head, kind)

            @pl.when(has_after)
            def _():
                hop_kv(head).start()

            @pl.when(odd == 0)
            def _():
                pair_kv(head, REACH).start()

        def pass_across(head):
            @pl.when(has_before & (odd == 1))
            def _():
                hop_kv(head).wait_recv()
                pair_kv(head, 0).start()

        def compute(head):
            chunks = span // ROWS

            def stacked(array, index):
                rows = pl.ds(index * ROWS, ROWS)
                return jnp.concatenate(
                    [
                        array[head, rows, member * HEAD_SIZE : (member + 1) * HEAD_SIZE]
                        for member in range(QUERY_PER_KV)
                    ],
                    axis=0,
                )

            def products(index):
                band = pl.ds(index * ROWS, span)
                scores = dot_last(window[head, 0, band, :], stacked(queries, index))
                top = jnp.full((8, QUERY_PER_KV * ROWS), -3e38, jnp.float32)
                for chunk in range(chunks):
                    here = pl.ds(chunk * ROWS, ROWS)
                    mask = bias[index, here, :]
                    score = scores[chunk * ROWS : (chunk + 1) * ROWS] + jnp.concatenate(
                        [mask] * QUERY_PER_KV, axis=1
                    )
                    score_buf[index, here, :] = score
                    top = jnp.maximum(top, folded(score, jnp.max))
                prob_grad_buf[index] = dot_last(
                    window[head, 1, band, :], stacked(cotangents, index)
                )
                return jnp.max(top, axis=0, keepdims=True)

            def soften(index, top):
                total = jnp.zeros((8, QUERY_PER_KV * ROWS), jnp.float32)
                delta = jnp.zeros((8, QUERY_PER_KV * ROWS), jnp.float32)
                for chunk in range(chunks):
                    here = pl.ds(chunk * ROWS, ROWS)
                    power = jnp.exp2((score_buf[index, here, :] - top) * exponent_scale)
                    score_buf[index, here, :] = power
                    total = total + folded(power, jnp.sum)
                    delta = delta + folded(power * prob_grad_buf[index, here, :], jnp.sum)
                inverse = 1.0 / jnp.sum(total, axis=0, keepdims=True)
                delta = jnp.sum(delta, axis=0, keepdims=True) * inverse
                for chunk in range(chunks):
                    here = pl.ds(chunk * ROWS, ROWS)
                    prob = score_buf[index, here, :] * inverse
                    score_grad = prob * (prob_grad_buf[index, here, :] - delta)
                    halves[index, 0, here, :] = score_grad.astype(jnp.bfloat16)
                    halves[index, 1, here, :] = prob.astype(jnp.bfloat16)

            def accumulate(index):
                for kind, array in enumerate((queries, cotangents)):
                    update = jnp.dot(
                        halves[index, kind],
                        stacked(array, index),
                        preferred_element_type=jnp.float32,
                    )
                    fresh = span - ROWS if index else 0
                    if index:
                        grads[head, kind, pl.ds(index * ROWS, fresh), :] += update[:fresh]
                    grads[head, kind, pl.ds(index * ROWS + fresh, span - fresh), :] = update[
                        fresh:
                    ]

            count = tokens // ROWS
            tops = [products(0)]
            for index in range(count):
                if index + 1 < count:
                    tops.append(products(index + 1))
                soften(index, tops[index])
                accumulate(index)

        def attend(head):
            @pl.when(has_before & (odd == 0))
            def _():
                hop_kv(head).wait_recv()

            @pl.when(has_before | (odd == 1))
            def _():
                pair_kv(head, REACH).wait_recv()

            compute(head)

            @pl.when(has_before | (odd == 1))
            def _():
                pair_grads(head).start()

        def send_back(head):
            @pl.when(has_before)
            def _():
                @pl.when(odd == 0)
                def _():
                    hop_out[head] = grads[head, :, block_rows(0), :].astype(jnp.bfloat16)

                @pl.when(odd == 1)
                def _():
                    pair_grads(head).wait_recv()
                    hop_out[head] = (grads[head, :, block_rows(0), :] + pair_in[head]).astype(
                        jnp.bfloat16
                    )

                hop_grads(head).start()

        def gather(head):
            @pl.when(odd == 0)
            def _():
                pair_grads(head).wait_recv()
                grads[head, :, block_rows(REACH), :] += pair_in[head]

            @pl.when(has_after)
            def _():
                hop_grads(head).wait_recv()
                grads[head, :, block_rows(REACH), :] += hop_in[head].astype(jnp.float32)

            owner = lax.rem(head, sections)

            @pl.when(owner != section)
            def _():
                part_out[head] = grads[head, :, block_rows(REACH), :].astype(jnp.bfloat16)
                part_copy(head, section, owner).start()

        @pl.loop(0, heads + AHEAD + 4)
        def _(step):
            def stage(lag, run):
                head = step - lag

                @pl.when((head >= 0) & (head < heads))
                def _():
                    run(head)

            def finish_own(head):
                @pl.when(lax.rem(head, sections) == section)
                def _():
                    finish(head)

            stage(0, pass_on)
            stage(1, pass_across)
            stage(AHEAD, attend)
            stage(AHEAD + 1, send_back)
            stage(AHEAD + 2, gather)
            stage(AHEAD + 3, finish_own)

    @pl.loop(0, heads)
    def _(head):
        owner = lax.rem(head, sections)
        for kind in range(2):

            @pl.when(owner == section)
            def _():
                store_copy(head, kind).wait()
                for step in range(1, sections):
                    spread_copy(head, kind, lax.rem(section + step, sections)).wait_send()

            @pl.when(owner != section)
            def _():
                spread_copy(head, kind, owner).wait_recv()


        @pl.when(cross)
        def _():
            ring_sent(head)

            @pl.when(has_after)
            def _():
                hop_kv(head).wait_send()

            @pl.when(has_before | (odd == 0))
            def _():
                pair_kv(head, REACH).wait_send()

            @pl.when(has_before | (odd == 1))
            def _():
                pair_grads(head).wait_send()

            @pl.when(has_before)
            def _():
                hop_grads(head).wait_send()

            @pl.when(owner != section)
            def _():
                part_copy(head, section, owner).wait_send()


def on_device(projected, grad_out, doc_lengths):
    sections = lax.axis_size("section")
    blocks = lax.axis_size("ctx")
    tokens = projected.shape[1]
    heads = KV_HEAD_COUNT
    slots = -(-heads // sections)
    span = REACH * tokens + ROWS
    window_rows = (REACH + 1) * tokens
    group_width = QUERY_PER_KV * HEAD_SIZE
    bf16, f32 = jnp.bfloat16, jnp.float32
    dma = pltpu.SemaphoreType.DMA
    return pl.pallas_call(
        functools.partial(kernel, sections, blocks),
        out_shape=jax.ShapeDtypeStruct((tokens, 2 * heads * HEAD_SIZE), bf16),
        in_specs=[
            pl.BlockSpec(memory_space=pltpu.SMEM),
            pl.BlockSpec(memory_space=pl.ANY),
            pl.BlockSpec(memory_space=pl.ANY),
        ],
        out_specs=pl.BlockSpec(memory_space=pl.ANY),
        scratch_shapes=[
            pltpu.VMEM((heads, tokens, group_width), bf16),
            pltpu.VMEM((heads, tokens, group_width), bf16),
            pltpu.VMEM((heads, 2, window_rows, HEAD_SIZE), bf16),
            pltpu.VMEM((tokens // ROWS, span, ROWS), f32),
            pltpu.VMEM((tokens // ROWS, span, QUERY_PER_KV * ROWS), f32),
            pltpu.VMEM((tokens // ROWS, span, QUERY_PER_KV * ROWS), f32),
            pltpu.VMEM((tokens // ROWS, 2, span, QUERY_PER_KV * ROWS), bf16),
            pltpu.VMEM((heads, 2, window_rows, HEAD_SIZE), f32),
            pltpu.VMEM((heads, 2, tokens, HEAD_SIZE), f32),
            pltpu.VMEM((heads, 2, tokens, HEAD_SIZE), bf16),
            pltpu.VMEM((heads, 2, tokens, HEAD_SIZE), bf16),
            pltpu.VMEM((heads, 2, tokens, HEAD_SIZE), bf16),
            pltpu.VMEM((slots, sections, 2, tokens, HEAD_SIZE), bf16),
            pltpu.VMEM((slots, 2, tokens, HEAD_SIZE), f32),
            pltpu.VMEM((slots, 2, tokens, HEAD_SIZE), bf16),
            dma((heads, 2)),
            dma((heads, 2, 2)),
            dma((heads, 2)),
            dma((heads,)),
            dma((heads,)),
            dma((heads,)),
            dma((heads,)),
            dma((heads,)),
            dma((heads,)),
            dma((heads,)),
            dma((heads,)),
            dma((heads,)),
            dma((slots, sections)),
            dma((slots, sections, 2)),
            dma((heads, 2)),
            dma((slots, 2)),
        ],
        compiler_params=pltpu.CompilerParams(
            collective_id=0, has_side_effects=True, vmem_limit_bytes=56 * 1024 * 1024
        ),
        cost_estimate=pl.CostEstimate(
            flops=10 * heads * tokens * group_width * span // 1,
            bytes_accessed=16 * tokens * heads * group_width,
            transcendentals=heads * QUERY_PER_KV * tokens * span,
        ),
    )(doc_lengths, projected[0], grad_out[0]).astype(f32)


def solution(mesh):
    return jax.shard_map(
        on_device,
        mesh=mesh,
        in_specs=(P("section", "ctx", None), P("section", "ctx", None), P()),
        out_specs=P("ctx", None),
        check_vma=False,
    )
```

```python
import functools
import math

import jax
import jax.numpy as jnp
from jax import lax
from jax.experimental import pallas as pl
from jax.experimental.pallas import tpu as pltpu
from jax.sharding import PartitionSpec as P

HEAD_SIZE = 128
KV_HEAD_COUNT = 8
QUERY_PER_KV = 3
REACH = 2
ROWS = 128
AHEAD = 2
MASKED_SCORE = -1e30
MESH = pl.DeviceIdType.MESH


def ring_swap(place, sections):
    half = sections // 2
    back = place // half
    return place * (1 - back) + back * (half + sections - 1 - place)


def dot_last(left, right):
    return lax.dot_general(
        left, right, (((1,), (1,)), ((), ())), preferred_element_type=jnp.float32
    )


def folded(value, reduce):
    return reduce(value.reshape(-1, 8, value.shape[-1]), axis=0)


def kernel(
    sections,
    blocks,
    lengths_ref,
    projected_ref,
    grad_out_ref,
    out_ref,
    queries,
    cotangents,
    window,
    bias,
    score_buf,
    prob_grad_buf,
    halves,
    grads,
    pair_in,
    hop_out,
    hop_in,
    part_out,
    part_in,
    final_half,
    load_sem,
    lend_send,
    lend_recv,
    ring_send,
    ring_recv,
    hop_kv_send,
    hop_kv_recv,
    pair_kv_send,
    pair_kv_recv,
    pair_send,
    pair_recv,
    hop_send,
    hop_recv,
    part_send,
    part_recv,
    spread_send,
    spread_recv,
    store_sem,
):
    section = lax.axis_index("section")
    block = lax.axis_index("ctx")
    odd = lax.rem(block, 2)
    partner = block + 1 - 2 * odd
    place = ring_swap(section, sections)
    heads = KV_HEAD_COUNT
    tokens = out_ref.shape[0]
    width = heads * HEAD_SIZE
    group_width = QUERY_PER_KV * HEAD_SIZE
    span = REACH * tokens + ROWS
    scale = 1.0 / math.sqrt(HEAD_SIZE)
    exponent_scale = scale * math.log2(math.e)
    cross = section > 0
    others = sections - 1
    lent = heads // sections
    kept = heads - lent
    at_home = jnp.where(section == 0, 1, 0)
    has_before = block >= REACH
    has_after = block + REACH < blocks

    def block_rows(index):
        return pl.ds(index * tokens, tokens)

    def load_shared(head, kind):
        return pltpu.make_async_copy(
            projected_ref.at[:, pl.ds(kind * width + head * HEAD_SIZE, HEAD_SIZE)],
            window.at[head, kind, block_rows(REACH), :],
            load_sem.at[head, kind],
        )

    def load_group(head, kind):
        source, target = ((projected_ref, queries), (grad_out_ref, cotangents))[kind]
        return pltpu.make_async_copy(
            source.at[:, pl.ds(head * group_width, group_width)],
            target.at[head],
            load_sem.at[head, kind],
        )

    def lend_copy(index, kind, source):
        origin, target = ((projected_ref, queries), (grad_out_ref, cotangents))[kind]
        unit = index * others + source - 1
        return pltpu.make_async_remote_copy(
            src_ref=origin.at[:, pl.ds((kept + index) * group_width, group_width)],
            dst_ref=target.at[unit],
            send_sem=lend_send.at[index, kind],
            recv_sem=lend_recv.at[unit, kind],
            device_id={"section": 0, "ctx": block},
            device_id_type=MESH,
        )

    def owner_of(head):
        return (1 - head // kept) * (1 + lax.rem(head, others))

    def ring_copy(head, kind, way):
        target_place = lax.rem(place + 1 - 2 * way + sections, sections)
        own = window.at[head, kind, block_rows(REACH), :]
        return pltpu.make_async_remote_copy(
            src_ref=own,
            dst_ref=own,
            send_sem=ring_send.at[head, kind, way],
            recv_sem=ring_recv.at[head, kind],
            device_id={"section": ring_swap(target_place, sections), "ctx": block},
            device_id_type=MESH,
        )

    def ring_sends(kind, way):
        middle = sections // 2
        if way == 0:
            return place < middle if kind == 0 else place + 1 < middle
        above = lax.rem(place - 1 + sections, sections)
        starts = (place == 0) | (place > middle)
        return starts & (above > middle if kind == 0 else above >= middle)

    def ring_start(head, kind):
        for way in range(2):

            @pl.when(ring_sends(kind, way))
            def _():
                ring_copy(head, kind, way).start()

    def ring_sent(head):
        for kind in range(2):
            for way in range(2):

                @pl.when(ring_sends(kind, way))
                def _():
                    ring_copy(head, kind, way).wait_send()

    def to_block(source, target, send_sem, recv_sem, target_block):
        return pltpu.make_async_remote_copy(
            src_ref=source,
            dst_ref=target,
            send_sem=send_sem,
            recv_sem=recv_sem,
            device_id={"section": section, "ctx": target_block},
            device_id_type=MESH,
        )

    def hop_kv(head):
        return to_block(
            window.at[head, :, block_rows(REACH), :],
            window.at[head, :, block_rows(0), :],
            hop_kv_send.at[head],
            hop_kv_recv.at[head],
            block + REACH,
        )

    def pair_kv(head, source_block):
        return to_block(
            window.at[head, :, block_rows(source_block), :],
            window.at[head, :, block_rows(1), :],
            pair_kv_send.at[head],
            pair_kv_recv.at[head],
            partner,
        )

    def pair_grads(head):
        return to_block(
            grads.at[head, :, block_rows(1), :],
            pair_in.at[head],
            pair_send.at[head],
            pair_recv.at[head],
            partner,
        )

    def hop_grads(head):
        return to_block(
            hop_out.at[head], hop_in.at[head], hop_send.at[head], hop_recv.at[head], block - REACH
        )

    def part_copy(head, source, target):
        return pltpu.make_async_remote_copy(
            src_ref=part_out.at[head],
            dst_ref=part_in.at[head // others, source],
            send_sem=part_send.at[head],
            recv_sem=part_recv.at[head // others, source],
            device_id={"section": target, "ctx": block},
            device_id_type=MESH,
        )

    def out_columns(head, kind):
        start = pl.multiple_of(kind * width + head * HEAD_SIZE, HEAD_SIZE)
        return out_ref.at[:, pl.ds(start, HEAD_SIZE)]

    def spread_copy(head, kind, target):
        return pltpu.make_async_remote_copy(
            src_ref=final_half.at[head, kind],
            dst_ref=out_columns(head, kind),
            send_sem=spread_send.at[head, target, kind],
            recv_sem=spread_recv.at[head, kind],
            device_id={"section": target, "ctx": block},
            device_id_type=MESH,
        )

    def store_copy(head, kind):
        return pltpu.make_async_copy(
            final_half.at[head, kind],
            out_columns(head, kind),
            store_sem.at[head, kind],
        )

    @pl.when(section == 0)
    def _():
        for head in range(heads):
            for kind in range(2):
                load_shared(head, kind).start()

    @pl.when(cross)
    def _():
        for head in range(kept):
            for kind in range(2):
                load_group(head, kind).start()

    barrier = pltpu.get_barrier_semaphore()
    for step in range(1, sections):
        pl.semaphore_signal(
            barrier,
            inc=1,
            device_id={"section": lax.rem(section + step, sections), "ctx": block},
            device_id_type=MESH,
        )
    pl.semaphore_signal(
        barrier, inc=1, device_id={"section": section, "ctx": partner}, device_id_type=MESH
    )

    @pl.when(has_before)
    def _():
        pl.semaphore_signal(
            barrier,
            inc=1,
            device_id={"section": section, "ctx": block - REACH},
            device_id_type=MESH,
        )

    @pl.when(has_after)
    def _():
        pl.semaphore_signal(
            barrier,
            inc=1,
            device_id={"section": section, "ctx": block + REACH},
            device_id_type=MESH,
        )

    before_count = jnp.where(has_before, 1, 0)
    after_count = jnp.where(has_after, 1, 0)
    pl.semaphore_wait(barrier, sections + before_count + after_count)

    def finish(head):
        own = block_rows(REACH)
        for source in range(1, sections):

            @pl.when(cross & (section != source))
            def _():
                part_copy(head, source, section).wait_recv()
                grads[head, :, own, :] += part_in[head // others, source].astype(jnp.float32)

        final_half[head, 0] = (grads[head, 0, own, :] * scale).astype(jnp.bfloat16)
        final_half[head, 1] = grads[head, 1, own, :].astype(jnp.bfloat16)
        for kind in range(2):
            store_copy(head, kind).start()
            for step in range(1, sections):
                spread_copy(head, kind, lax.rem(section + step, sections)).start()

    def pass_across(head):
        @pl.when(has_before & (odd == 1))
        def _():
            hop_kv(head).wait_recv()
            pair_kv(head, 0).start()

    def to_later(head):
        @pl.when(has_after)
        def _():
            hop_kv(head).start()

        @pl.when(odd == 0)
        def _():
            pair_kv(head, REACH).start()

    @pl.when(section == 0)
    def _():
        for head in range(heads):
            for kind in range(2):
                load_shared(head, kind).wait()
        for head in range(min(3, kept)):
            for kind in range(2):
                ring_start(head, kind)
        for head in range(kept, heads):
            to_later(head)

    @pl.when(cross)
    def _():
        for index in range(lent):
            for kind in range(2):
                lend_copy(index, kind, section).start()

    for index in range(tokens // ROWS):
        query_place = block * tokens + index * ROWS + lax.broadcasted_iota(
            jnp.int32, (8, ROWS), 1
        )
        start = jnp.zeros((8, ROWS), jnp.int32)
        end = 0
        for document in range(lengths_ref.shape[0]):
            end = end + lengths_ref[document]
            start = jnp.where(query_place >= end, end, start)
        key_place = (
            (block - REACH) * tokens
            + index * ROWS
            + lax.broadcasted_iota(jnp.int32, (span, ROWS), 0)
        )
        allowed = (key_place >= start[:1]) & (key_place <= query_place[:1])
        bias[index] = jnp.where(allowed, 0.0, MASKED_SCORE)

    @pl.loop(0, heads)
    def _(head):
        grads[head] = jnp.zeros(grads.shape[1:], jnp.float32)

        @pl.when(block < REACH)
        def _():
            window[head, :, block_rows(0), :] = jnp.zeros((2, tokens, HEAD_SIZE), jnp.bfloat16)

        @pl.when(block == 0)
        def _():
            window[head, :, block_rows(1), :] = jnp.zeros((2, tokens, HEAD_SIZE), jnp.bfloat16)

    @pl.when(section == 0)
    def _():
        for head in range(min(3, kept), kept):
            for kind in range(2):
                ring_start(head, kind)
        for head in range(kept, heads):
            pass_across(head)

    @pl.when(cross)
    def _():
        for head in range(kept):
            for kind in range(2):
                load_group(head, kind).wait()

    def pass_on(head):
        for kind in range(2):
            ring_copy(head, kind, 0).wait_recv()
            ring_start(head, kind)

        to_later(head)

    def compute(unit, head):
        chunks = span // ROWS

        def stacked(array, index):
            rows = pl.ds(index * ROWS, ROWS)
            return jnp.concatenate(
                [
                    array[unit, rows, member * HEAD_SIZE : (member + 1) * HEAD_SIZE]
                    for member in range(QUERY_PER_KV)
                ],
                axis=0,
            )

        def products(index):
            band = pl.ds(index * ROWS, span)
            scores = dot_last(window[head, 0, band, :], stacked(queries, index))
            top = jnp.full((8, QUERY_PER_KV * ROWS), -3e38, jnp.float32)
            for chunk in range(chunks):
                here = pl.ds(chunk * ROWS, ROWS)
                mask = bias[index, here, :]
                score = scores[chunk * ROWS : (chunk + 1) * ROWS] + jnp.concatenate(
                    [mask] * QUERY_PER_KV, axis=1
                )
                score_buf[index, here, :] = score
                top = jnp.maximum(top, folded(score, jnp.max))
            prob_grad_buf[index] = dot_last(
                window[head, 1, band, :], stacked(cotangents, index)
            )
            return jnp.max(top, axis=0, keepdims=True)

        def soften(index, top):
            total = jnp.zeros((8, QUERY_PER_KV * ROWS), jnp.float32)
            delta = jnp.zeros((8, QUERY_PER_KV * ROWS), jnp.float32)
            for chunk in range(chunks):
                here = pl.ds(chunk * ROWS, ROWS)
                power = jnp.exp2((score_buf[index, here, :] - top) * exponent_scale)
                score_buf[index, here, :] = power
                total = total + folded(power, jnp.sum)
                delta = delta + folded(power * prob_grad_buf[index, here, :], jnp.sum)
            inverse = 1.0 / jnp.sum(total, axis=0, keepdims=True)
            delta = jnp.sum(delta, axis=0, keepdims=True) * inverse
            for chunk in range(chunks):
                here = pl.ds(chunk * ROWS, ROWS)
                prob = score_buf[index, here, :] * inverse
                score_grad = prob * (prob_grad_buf[index, here, :] - delta)
                halves[index, 0, here, :] = score_grad.astype(jnp.bfloat16)
                halves[index, 1, here, :] = prob.astype(jnp.bfloat16)

        def accumulate(index):
            for kind, array in enumerate((queries, cotangents)):
                update = jnp.dot(
                    halves[index, kind],
                    stacked(array, index),
                    preferred_element_type=jnp.float32,
                )
                grads[head, kind, pl.ds(index * ROWS, span), :] += update

        count = tokens // ROWS
        tops = [products(0)]
        for index in range(count):
            if index + 1 < count:
                tops.append(products(index + 1))
            soften(index, tops[index])
            accumulate(index)

    def head_of(unit):
        return (1 - at_home) * unit + at_home * (kept + unit // others)

    def attend(unit):
        head = head_of(unit)
        first = cross | (lax.rem(unit, others) == 0)
        last = cross | (lax.rem(unit, others) == others - 1)

        @pl.when(section == 0)
        def _():
            for kind in range(2):
                lend_copy(unit // others, kind, 1 + lax.rem(unit, others)).wait_recv()

        @pl.when(first & has_before & (odd == 0))
        def _():
            hop_kv(head).wait_recv()

        @pl.when(first & (has_before | (odd == 1)))
        def _():
            pair_kv(head, REACH).wait_recv()

        compute(unit, head)

        @pl.when(last & (has_before | (odd == 1)))
        def _():
            pair_grads(head).start()

    def send_back(head):
        @pl.when(has_before)
        def _():
            @pl.when(odd == 0)
            def _():
                hop_out[head] = grads[head, :, block_rows(0), :].astype(jnp.bfloat16)

            @pl.when(odd == 1)
            def _():
                pair_grads(head).wait_recv()
                hop_out[head] = (grads[head, :, block_rows(0), :] + pair_in[head]).astype(
                    jnp.bfloat16
                )

            hop_grads(head).start()

    def gather(head):
        @pl.when(odd == 0)
        def _():
            pair_grads(head).wait_recv()
            grads[head, :, block_rows(REACH), :] += pair_in[head]

        @pl.when(has_after)
        def _():
            hop_grads(head).wait_recv()
            grads[head, :, block_rows(REACH), :] += hop_in[head].astype(jnp.float32)

        owner = owner_of(head)

        @pl.when(owner != section)
        def _():
            part_out[head] = grads[head, :, block_rows(REACH), :].astype(jnp.bfloat16)
            part_copy(head, section, owner).start()

    @pl.loop(0, kept + AHEAD + 4)
    def _(step):
        def stage(lag, run):
            unit = step - lag

            @pl.when((unit >= 0) & (unit < kept))
            def _():
                run(unit)

        def when_summed(run):
            def staged(unit):
                @pl.when(cross | (lax.rem(unit, others) == others - 1))
                def _():
                    run(head_of(unit))

            return staged

        def when_cross(run):
            def staged(unit):
                @pl.when(cross)
                def _():
                    run(unit)

            return staged

        def finish_own(head):
            @pl.when(owner_of(head) == section)
            def _():
                finish(head)

        stage(0, when_cross(pass_on))
        stage(1, when_cross(pass_across))
        stage(AHEAD, attend)
        stage(AHEAD + 1, when_summed(send_back))
        stage(AHEAD + 2, when_summed(gather))
        stage(AHEAD + 3, when_summed(finish_own))

    @pl.loop(0, heads)
    def _(head):
        owner = owner_of(head)
        home = head // kept
        for kind in range(2):

            @pl.when(owner == section)
            def _():
                store_copy(head, kind).wait()
                for step in range(1, sections):
                    spread_copy(head, kind, lax.rem(section + step, sections)).wait_send()

            @pl.when(owner != section)
            def _():
                spread_copy(head, kind, owner).wait_recv()


        @pl.when(home == 0)
        def _():
            ring_sent(head)

        @pl.when(cross & (home == 1))
        def _():
            for kind in range(2):
                lend_copy(head - kept, kind, section).wait_send()

        @pl.when(home == at_home)
        def _():
            @pl.when(has_after)
            def _():
                hop_kv(head).wait_send()

            @pl.when(has_before | (odd == 0))
            def _():
                pair_kv(head, REACH).wait_send()

            @pl.when(has_before | (odd == 1))
            def _():
                pair_grads(head).wait_send()

            @pl.when(has_before)
            def _():
                hop_grads(head).wait_send()

            @pl.when(owner != section)
            def _():
                part_copy(head, section, owner).wait_send()


def on_device(projected, grad_out, doc_lengths):
    sections = lax.axis_size("section")
    blocks = lax.axis_size("ctx")
    tokens = projected.shape[1]
    heads = KV_HEAD_COUNT
    lent = heads // sections
    kept = heads - lent
    span = REACH * tokens + ROWS
    window_rows = (REACH + 1) * tokens
    group_width = QUERY_PER_KV * HEAD_SIZE
    bf16, f32 = jnp.bfloat16, jnp.float32
    dma = pltpu.SemaphoreType.DMA
    return pl.pallas_call(
        functools.partial(kernel, sections, blocks),
        out_shape=jax.ShapeDtypeStruct((tokens, 2 * heads * HEAD_SIZE), bf16),
        in_specs=[
            pl.BlockSpec(memory_space=pltpu.SMEM),
            pl.BlockSpec(memory_space=pl.ANY),
            pl.BlockSpec(memory_space=pl.ANY),
        ],
        out_specs=pl.BlockSpec(memory_space=pl.ANY),
        scratch_shapes=[
            pltpu.VMEM((kept, tokens, group_width), bf16),
            pltpu.VMEM((kept, tokens, group_width), bf16),
            pltpu.VMEM((heads, 2, window_rows, HEAD_SIZE), bf16),
            pltpu.VMEM((tokens // ROWS, span, ROWS), f32),
            pltpu.VMEM((tokens // ROWS, span, QUERY_PER_KV * ROWS), f32),
            pltpu.VMEM((tokens // ROWS, span, QUERY_PER_KV * ROWS), f32),
            pltpu.VMEM((tokens // ROWS, 2, span, QUERY_PER_KV * ROWS), bf16),
            pltpu.VMEM((heads, 2, window_rows, HEAD_SIZE), f32),
            pltpu.VMEM((heads, 2, tokens, HEAD_SIZE), f32),
            pltpu.VMEM((heads, 2, tokens, HEAD_SIZE), bf16),
            pltpu.VMEM((heads, 2, tokens, HEAD_SIZE), bf16),
            pltpu.VMEM((heads, 2, tokens, HEAD_SIZE), bf16),
            pltpu.VMEM((lent, sections, 2, tokens, HEAD_SIZE), bf16),
            pltpu.VMEM((heads, 2, tokens, HEAD_SIZE), bf16),
            dma((heads, 2)),
            dma((lent, 2)),
            dma((kept, 2)),
            dma((heads, 2, 2)),
            dma((heads, 2)),
            dma((heads,)),
            dma((heads,)),
            dma((heads,)),
            dma((heads,)),
            dma((heads,)),
            dma((heads,)),
            dma((heads,)),
            dma((heads,)),
            dma((heads,)),
            dma((lent, sections)),
            dma((heads, sections, 2)),
            dma((heads, 2)),
            dma((heads, 2)),
        ],
        compiler_params=pltpu.CompilerParams(
            collective_id=0, has_side_effects=True, vmem_limit_bytes=56 * 1024 * 1024
        ),
        cost_estimate=pl.CostEstimate(
            flops=10 * heads * tokens * group_width * span // 1,
            bytes_accessed=16 * tokens * heads * group_width,
            transcendentals=heads * QUERY_PER_KV * tokens * span,
        ),
    )(doc_lengths, projected[0], grad_out[0]).astype(f32)


def solution(mesh):
    return jax.shard_map(
        on_device,
        mesh=mesh,
        in_specs=(P("section", "ctx", None), P("section", "ctx", None), P()),
        out_specs=P("ctx", None),
        check_vma=False,
    )
```

```python
import functools
import math

import jax
import jax.numpy as jnp
from jax import lax
from jax.experimental import pallas as pl
from jax.experimental.pallas import tpu as pltpu
from jax.sharding import PartitionSpec as P

HEAD_SIZE = 128
KV_HEAD_COUNT = 8
QUERY_PER_KV = 3
REACH = 2
ROWS = 128
AHEAD = 2
MASKED_SCORE = -1e30
MESH = pl.DeviceIdType.MESH


def ring_swap(place, sections):
    half = sections // 2
    back = place // half
    return place * (1 - back) + back * (half + sections - 1 - place)


def dot_last(left, right):
    return lax.dot_general(
        left, right, (((1,), (1,)), ((), ())), preferred_element_type=jnp.float32
    )


def folded(value, reduce):
    return reduce(value.reshape(-1, 8, value.shape[-1]), axis=0)


def kernel(
    sections,
    blocks,
    lengths_ref,
    projected_ref,
    grad_out_ref,
    out_ref,
    queries,
    cotangents,
    window,
    bias,
    score_buf,
    prob_grad_buf,
    halves,
    grads,
    pair_in,
    hop_out,
    hop_in,
    part_out,
    part_in,
    final_half,
    load_sem,
    lend_send,
    lend_recv,
    ring_send,
    ring_recv,
    hop_kv_send,
    hop_kv_recv,
    pair_kv_send,
    pair_kv_recv,
    pair_send,
    pair_recv,
    hop_send,
    hop_recv,
    part_send,
    part_recv,
    spread_send,
    spread_recv,
    store_sem,
):
    section = lax.axis_index("section")
    block = lax.axis_index("ctx")
    odd = lax.rem(block, 2)
    partner = block + 1 - 2 * odd
    place = ring_swap(section, sections)
    heads = KV_HEAD_COUNT
    tokens = out_ref.shape[0]
    width = heads * HEAD_SIZE
    group_width = QUERY_PER_KV * HEAD_SIZE
    span = REACH * tokens + ROWS
    scale = 1.0 / math.sqrt(HEAD_SIZE)
    exponent_scale = scale * math.log2(math.e)
    cross = section > 0
    others = sections - 1
    lent = heads // sections
    kept = heads - lent
    at_home = jnp.where(section == 0, 1, 0)
    has_before = block >= REACH
    has_after = block + REACH < blocks

    def block_rows(index):
        return pl.ds(index * tokens, tokens)

    def load_shared(head, kind):
        return pltpu.make_async_copy(
            projected_ref.at[:, pl.ds(kind * width + head * HEAD_SIZE, HEAD_SIZE)],
            window.at[head, kind, block_rows(REACH), :],
            load_sem.at[head, kind],
        )

    def load_group(head, kind):
        source, target = ((projected_ref, queries), (grad_out_ref, cotangents))[kind]
        return pltpu.make_async_copy(
            source.at[:, pl.ds(head * group_width, group_width)],
            target.at[head],
            load_sem.at[head, kind],
        )

    def lend_copy(index, kind, source):
        origin, target = ((projected_ref, queries), (grad_out_ref, cotangents))[kind]
        unit = index * others + source - 1
        return pltpu.make_async_remote_copy(
            src_ref=origin.at[:, pl.ds((kept + index) * group_width, group_width)],
            dst_ref=target.at[unit],
            send_sem=lend_send.at[index, kind],
            recv_sem=lend_recv.at[unit, kind],
            device_id={"section": 0, "ctx": block},
            device_id_type=MESH,
        )

    def owner_of(head):
        return (1 - head // kept) * (1 + lax.rem(head, others))

    def ring_copy(head, kind, way):
        target_place = lax.rem(place + 1 - 2 * way + sections, sections)
        own = window.at[head, kind, block_rows(REACH), :]
        return pltpu.make_async_remote_copy(
            src_ref=own,
            dst_ref=own,
            send_sem=ring_send.at[head, kind, way],
            recv_sem=ring_recv.at[head, kind],
            device_id={"section": ring_swap(target_place, sections), "ctx": block},
            device_id_type=MESH,
        )

    def ring_sends(kind, way):
        middle = sections // 2
        if way == 0:
            return place < middle if kind == 0 else place + 1 < middle
        above = lax.rem(place - 1 + sections, sections)
        starts = (place == 0) | (place > middle)
        return starts & (above > middle if kind == 0 else above >= middle)

    def ring_start(head, kind):
        for way in range(2):

            @pl.when(ring_sends(kind, way))
            def _():
                ring_copy(head, kind, way).start()

    def ring_sent(head):
        for kind in range(2):
            for way in range(2):

                @pl.when(ring_sends(kind, way))
                def _():
                    ring_copy(head, kind, way).wait_send()

    def to_block(source, target, send_sem, recv_sem, target_block):
        return pltpu.make_async_remote_copy(
            src_ref=source,
            dst_ref=target,
            send_sem=send_sem,
            recv_sem=recv_sem,
            device_id={"section": section, "ctx": target_block},
            device_id_type=MESH,
        )

    def hop_kv(head):
        return to_block(
            window.at[head, :, block_rows(REACH), :],
            window.at[head, :, block_rows(0), :],
            hop_kv_send.at[head],
            hop_kv_recv.at[head],
            block + REACH,
        )

    def pair_kv(head, source_block):
        return to_block(
            window.at[head, :, block_rows(source_block), :],
            window.at[head, :, block_rows(1), :],
            pair_kv_send.at[head],
            pair_kv_recv.at[head],
            partner,
        )

    def pair_grads(head):
        return to_block(
            grads.at[head, :, block_rows(1), :],
            pair_in.at[head],
            pair_send.at[head],
            pair_recv.at[head],
            partner,
        )

    def hop_grads(head, kind):
        return to_block(
            hop_out.at[head, kind],
            hop_in.at[head, kind],
            hop_send.at[head, kind],
            hop_recv.at[head, kind],
            block - REACH,
        )

    def part_copy(head, kind, source, target):
        return pltpu.make_async_remote_copy(
            src_ref=part_out.at[head, kind],
            dst_ref=part_in.at[head // others, source, kind],
            send_sem=part_send.at[head, kind],
            recv_sem=part_recv.at[head // others, source, kind],
            device_id={"section": target, "ctx": block},
            device_id_type=MESH,
        )

    def out_columns(head, kind):
        start = pl.multiple_of(kind * width + head * HEAD_SIZE, HEAD_SIZE)
        return out_ref.at[:, pl.ds(start, HEAD_SIZE)]

    def spread_copy(head, kind, target):
        return pltpu.make_async_remote_copy(
            src_ref=final_half.at[head, kind],
            dst_ref=out_columns(head, kind),
            send_sem=spread_send.at[head, target, kind],
            recv_sem=spread_recv.at[head, kind],
            device_id={"section": target, "ctx": block},
            device_id_type=MESH,
        )

    def store_copy(head, kind):
        return pltpu.make_async_copy(
            final_half.at[head, kind],
            out_columns(head, kind),
            store_sem.at[head, kind],
        )

    @pl.when(section == 0)
    def _():
        for head in range(heads):
            for kind in range(2):
                load_shared(head, kind).start()

    @pl.when(cross)
    def _():
        for head in range(kept):
            for kind in range(2):
                load_group(head, kind).start()

    barrier = pltpu.get_barrier_semaphore()
    for step in range(1, sections):
        pl.semaphore_signal(
            barrier,
            inc=1,
            device_id={"section": lax.rem(section + step, sections), "ctx": block},
            device_id_type=MESH,
        )
    pl.semaphore_signal(
        barrier, inc=1, device_id={"section": section, "ctx": partner}, device_id_type=MESH
    )

    @pl.when(has_before)
    def _():
        pl.semaphore_signal(
            barrier,
            inc=1,
            device_id={"section": section, "ctx": block - REACH},
            device_id_type=MESH,
        )

    @pl.when(has_after)
    def _():
        pl.semaphore_signal(
            barrier,
            inc=1,
            device_id={"section": section, "ctx": block + REACH},
            device_id_type=MESH,
        )

    before_count = jnp.where(has_before, 1, 0)
    after_count = jnp.where(has_after, 1, 0)
    pl.semaphore_wait(barrier, sections + before_count + after_count)

    def finish(head):
        own = block_rows(REACH)
        for kind in range(2):
            for source in range(1, sections):

                @pl.when(cross & (section != source))
                def _():
                    part_copy(head, kind, source, section).wait_recv()
                    grads[head, kind, own, :] += part_in[head // others, source, kind].astype(
                        jnp.float32
                    )

            total = grads[head, kind, own, :]
            if kind == 0:
                total = total * scale
            final_half[head, kind] = total.astype(jnp.bfloat16)
            store_copy(head, kind).start()
            for step in range(1, sections):
                spread_copy(head, kind, lax.rem(section + step, sections)).start()

    def pass_across(head):
        @pl.when(has_before & (odd == 1))
        def _():
            hop_kv(head).wait_recv()
            pair_kv(head, 0).start()

    def to_later(head):
        @pl.when(has_after)
        def _():
            hop_kv(head).start()

        @pl.when(odd == 0)
        def _():
            pair_kv(head, REACH).start()

    @pl.when(section == 0)
    def _():
        for head in range(min(3, kept)):
            for kind in range(2):
                load_shared(head, kind).wait()
                ring_start(head, kind)
        for head in range(min(3, kept), heads):
            for kind in range(2):
                load_shared(head, kind).wait()
        for head in range(kept, heads):
            to_later(head)

    @pl.when(cross)
    def _():
        for index in range(lent):
            for kind in range(2):
                lend_copy(index, kind, section).start()

    for index in range(tokens // ROWS):
        query_place = block * tokens + index * ROWS + lax.broadcasted_iota(
            jnp.int32, (8, ROWS), 1
        )
        start = jnp.zeros((8, ROWS), jnp.int32)
        end = 0
        for document in range(lengths_ref.shape[0]):
            end = end + lengths_ref[document]
            start = jnp.where(query_place >= end, end, start)
        key_place = (
            (block - REACH) * tokens
            + index * ROWS
            + lax.broadcasted_iota(jnp.int32, (span, ROWS), 0)
        )
        allowed = (key_place >= start[:1]) & (key_place <= query_place[:1])
        bias[index] = jnp.where(allowed, 0.0, MASKED_SCORE)

    @pl.loop(0, heads)
    def _(head):
        grads[head] = jnp.zeros(grads.shape[1:], jnp.float32)

        @pl.when(block < REACH)
        def _():
            window[head, :, block_rows(0), :] = jnp.zeros((2, tokens, HEAD_SIZE), jnp.bfloat16)

        @pl.when(block == 0)
        def _():
            window[head, :, block_rows(1), :] = jnp.zeros((2, tokens, HEAD_SIZE), jnp.bfloat16)

    @pl.when(section == 0)
    def _():
        for head in range(min(3, kept), kept):
            for kind in range(2):
                ring_start(head, kind)
        for head in range(kept, heads):
            pass_across(head)

    @pl.when(cross)
    def _():
        for head in range(kept):
            for kind in range(2):
                load_group(head, kind).wait()

    def pass_on(head):
        for kind in range(2):
            ring_copy(head, kind, 0).wait_recv()
            ring_start(head, kind)

        to_later(head)

    def compute(unit, head):
        chunks = span // ROWS

        def stacked(array, index):
            rows = pl.ds(index * ROWS, ROWS)
            return jnp.concatenate(
                [
                    array[unit, rows, member * HEAD_SIZE : (member + 1) * HEAD_SIZE]
                    for member in range(QUERY_PER_KV)
                ],
                axis=0,
            )

        def products(index):
            band = pl.ds(index * ROWS, span)
            scores = dot_last(window[head, 0, band, :], stacked(queries, index))
            top = jnp.full((8, QUERY_PER_KV * ROWS), -3e38, jnp.float32)
            for chunk in range(chunks):
                here = pl.ds(chunk * ROWS, ROWS)
                mask = bias[index, here, :]
                score = scores[chunk * ROWS : (chunk + 1) * ROWS] + jnp.concatenate(
                    [mask] * QUERY_PER_KV, axis=1
                )
                score_buf[index, here, :] = score
                top = jnp.maximum(top, folded(score, jnp.max))
            prob_grad_buf[index] = dot_last(
                window[head, 1, band, :], stacked(cotangents, index)
            )
            return jnp.max(top, axis=0, keepdims=True)

        def soften(index, top):
            total = jnp.zeros((8, QUERY_PER_KV * ROWS), jnp.float32)
            delta = jnp.zeros((8, QUERY_PER_KV * ROWS), jnp.float32)
            for chunk in range(chunks):
                here = pl.ds(chunk * ROWS, ROWS)
                power = jnp.exp2((score_buf[index, here, :] - top) * exponent_scale)
                score_buf[index, here, :] = power
                total = total + folded(power, jnp.sum)
                delta = delta + folded(power * prob_grad_buf[index, here, :], jnp.sum)
            inverse = 1.0 / jnp.sum(total, axis=0, keepdims=True)
            delta = jnp.sum(delta, axis=0, keepdims=True) * inverse
            for chunk in range(chunks):
                here = pl.ds(chunk * ROWS, ROWS)
                prob = score_buf[index, here, :] * inverse
                score_grad = prob * (prob_grad_buf[index, here, :] - delta)
                halves[index, 0, here, :] = score_grad.astype(jnp.bfloat16)
                halves[index, 1, here, :] = prob.astype(jnp.bfloat16)

        def accumulate(index):
            for kind, array in enumerate((queries, cotangents)):
                update = jnp.dot(
                    halves[index, kind],
                    stacked(array, index),
                    preferred_element_type=jnp.float32,
                )
                grads[head, kind, pl.ds(index * ROWS, span), :] += update

        count = tokens // ROWS
        tops = [products(0)]
        for index in range(count):
            if index + 1 < count:
                tops.append(products(index + 1))
            soften(index, tops[index])
            accumulate(index)

    def head_of(unit):
        return (1 - at_home) * unit + at_home * (kept + unit // others)

    def attend(unit):
        head = head_of(unit)
        first = cross | (lax.rem(unit, others) == 0)
        last = cross | (lax.rem(unit, others) == others - 1)

        @pl.when(section == 0)
        def _():
            for kind in range(2):
                lend_copy(unit // others, kind, 1 + lax.rem(unit, others)).wait_recv()

        @pl.when(first & has_before & (odd == 0))
        def _():
            hop_kv(head).wait_recv()

        @pl.when(first & (has_before | (odd == 1)))
        def _():
            pair_kv(head, REACH).wait_recv()

        compute(unit, head)

        @pl.when(last & (has_before | (odd == 1)))
        def _():
            pair_grads(head).start()

    def send_back(head):
        @pl.when(has_before)
        def _():
            @pl.when(odd == 1)
            def _():
                pair_grads(head).wait_recv()

            for kind in range(2):

                @pl.when(odd == 0)
                def _():
                    hop_out[head, kind] = grads[head, kind, block_rows(0), :].astype(jnp.bfloat16)

                @pl.when(odd == 1)
                def _():
                    hop_out[head, kind] = (
                        grads[head, kind, block_rows(0), :] + pair_in[head, kind]
                    ).astype(jnp.bfloat16)

                hop_grads(head, kind).start()

    def gather(head):
        owner = owner_of(head)

        @pl.when(odd == 0)
        def _():
            pair_grads(head).wait_recv()
            grads[head, :, block_rows(REACH), :] += pair_in[head]

        for kind in range(2):

            @pl.when(has_after)
            def _():
                hop_grads(head, kind).wait_recv()
                grads[head, kind, block_rows(REACH), :] += hop_in[head, kind].astype(jnp.float32)

            @pl.when(owner != section)
            def _():
                part_out[head, kind] = grads[head, kind, block_rows(REACH), :].astype(jnp.bfloat16)
                part_copy(head, kind, section, owner).start()

    @pl.loop(0, kept + AHEAD + 4)
    def _(step):
        def stage(lag, run):
            unit = step - lag

            @pl.when((unit >= 0) & (unit < kept))
            def _():
                run(unit)

        def when_summed(run):
            def staged(unit):
                @pl.when(cross | (lax.rem(unit, others) == others - 1))
                def _():
                    run(head_of(unit))

            return staged

        def when_cross(run):
            def staged(unit):
                @pl.when(cross)
                def _():
                    run(unit)

            return staged

        def finish_own(head):
            @pl.when(owner_of(head) == section)
            def _():
                finish(head)

        stage(0, when_cross(pass_on))
        stage(1, when_cross(pass_across))
        stage(AHEAD, attend)
        stage(AHEAD + 1, when_summed(send_back))
        stage(AHEAD + 2, when_summed(gather))
        stage(AHEAD + 3, when_summed(finish_own))

    @pl.loop(0, heads)
    def _(head):
        owner = owner_of(head)
        home = head // kept
        for kind in range(2):

            @pl.when(owner == section)
            def _():
                store_copy(head, kind).wait()
                for step in range(1, sections):
                    spread_copy(head, kind, lax.rem(section + step, sections)).wait_send()

            @pl.when(owner != section)
            def _():
                spread_copy(head, kind, owner).wait_recv()


        @pl.when(home == 0)
        def _():
            ring_sent(head)

        @pl.when(cross & (home == 1))
        def _():
            for kind in range(2):
                lend_copy(head - kept, kind, section).wait_send()

        @pl.when(home == at_home)
        def _():
            @pl.when(has_after)
            def _():
                hop_kv(head).wait_send()

            @pl.when(has_before | (odd == 0))
            def _():
                pair_kv(head, REACH).wait_send()

            @pl.when(has_before | (odd == 1))
            def _():
                pair_grads(head).wait_send()

            @pl.when(has_before)
            def _():
                for kind in range(2):
                    hop_grads(head, kind).wait_send()

            @pl.when(owner != section)
            def _():
                for kind in range(2):
                    part_copy(head, kind, section, owner).wait_send()


def on_device(projected, grad_out, doc_lengths):
    sections = lax.axis_size("section")
    blocks = lax.axis_size("ctx")
    tokens = projected.shape[1]
    heads = KV_HEAD_COUNT
    lent = heads // sections
    kept = heads - lent
    span = REACH * tokens + ROWS
    window_rows = (REACH + 1) * tokens
    group_width = QUERY_PER_KV * HEAD_SIZE
    bf16, f32 = jnp.bfloat16, jnp.float32
    dma = pltpu.SemaphoreType.DMA
    return pl.pallas_call(
        functools.partial(kernel, sections, blocks),
        out_shape=jax.ShapeDtypeStruct((tokens, 2 * heads * HEAD_SIZE), bf16),
        in_specs=[
            pl.BlockSpec(memory_space=pltpu.SMEM),
            pl.BlockSpec(memory_space=pl.ANY),
            pl.BlockSpec(memory_space=pl.ANY),
        ],
        out_specs=pl.BlockSpec(memory_space=pl.ANY),
        scratch_shapes=[
            pltpu.VMEM((kept, tokens, group_width), bf16),
            pltpu.VMEM((kept, tokens, group_width), bf16),
            pltpu.VMEM((heads, 2, window_rows, HEAD_SIZE), bf16),
            pltpu.VMEM((tokens // ROWS, span, ROWS), f32),
            pltpu.VMEM((tokens // ROWS, span, QUERY_PER_KV * ROWS), f32),
            pltpu.VMEM((tokens // ROWS, span, QUERY_PER_KV * ROWS), f32),
            pltpu.VMEM((tokens // ROWS, 2, span, QUERY_PER_KV * ROWS), bf16),
            pltpu.VMEM((heads, 2, window_rows, HEAD_SIZE), f32),
            pltpu.VMEM((heads, 2, tokens, HEAD_SIZE), f32),
            pltpu.VMEM((heads, 2, tokens, HEAD_SIZE), bf16),
            pltpu.VMEM((heads, 2, tokens, HEAD_SIZE), bf16),
            pltpu.VMEM((heads, 2, tokens, HEAD_SIZE), bf16),
            pltpu.VMEM((lent, sections, 2, tokens, HEAD_SIZE), bf16),
            pltpu.VMEM((heads, 2, tokens, HEAD_SIZE), bf16),
            dma((heads, 2)),
            dma((lent, 2)),
            dma((kept, 2)),
            dma((heads, 2, 2)),
            dma((heads, 2)),
            dma((heads,)),
            dma((heads,)),
            dma((heads,)),
            dma((heads,)),
            dma((heads,)),
            dma((heads,)),
            dma((heads, 2)),
            dma((heads, 2)),
            dma((heads, 2)),
            dma((lent, sections, 2)),
            dma((heads, sections, 2)),
            dma((heads, 2)),
            dma((heads, 2)),
        ],
        compiler_params=pltpu.CompilerParams(
            collective_id=0, has_side_effects=True, vmem_limit_bytes=56 * 1024 * 1024
        ),
        cost_estimate=pl.CostEstimate(
            flops=10 * heads * tokens * group_width * span // 1,
            bytes_accessed=16 * tokens * heads * group_width,
            transcendentals=heads * QUERY_PER_KV * tokens * span,
        ),
    )(doc_lengths, projected[0], grad_out[0]).astype(f32)


def solution(mesh):
    return jax.shard_map(
        on_device,
        mesh=mesh,
        in_specs=(P("section", "ctx", None), P("section", "ctx", None), P()),
        out_specs=P("ctx", None),
        check_vma=False,
    )
```

```python
import functools
import math

import jax
import jax.numpy as jnp
from jax import lax
from jax.experimental import pallas as pl
from jax.experimental.pallas import tpu as pltpu
from jax.sharding import PartitionSpec as P

HEAD_SIZE = 128
KV_HEAD_COUNT = 8
QUERY_PER_KV = 3
REACH = 2
ROWS = 128
AHEAD = 2
MASKED_SCORE = -1e30
MESH = pl.DeviceIdType.MESH


def ring_swap(place, sections):
    half = sections // 2
    back = place // half
    return place * (1 - back) + back * (half + sections - 1 - place)


def dot_last(left, right):
    return lax.dot_general(
        left, right, (((1,), (1,)), ((), ())), preferred_element_type=jnp.float32
    )


def folded(value, reduce):
    return reduce(value.reshape(-1, 8, value.shape[-1]), axis=0)


def kernel(
    sections,
    blocks,
    lengths_ref,
    projected_ref,
    grad_out_ref,
    out_ref,
    queries,
    cotangents,
    window,
    bias,
    score_buf,
    prob_grad_buf,
    halves,
    grads,
    pair_in,
    hop_out,
    hop_in,
    part_out,
    part_in,
    final_half,
    load_sem,
    lend_send,
    lend_recv,
    ring_send,
    ring_recv,
    hop_kv_send,
    hop_kv_recv,
    pair_kv_send,
    pair_kv_recv,
    pair_send,
    pair_recv,
    hop_send,
    hop_recv,
    part_send,
    part_recv,
    spread_send,
    spread_recv,
    store_sem,
):
    section = lax.axis_index("section")
    block = lax.axis_index("ctx")
    odd = lax.rem(block, 2)
    partner = block + 1 - 2 * odd
    place = ring_swap(section, sections)
    heads = KV_HEAD_COUNT
    tokens = out_ref.shape[0]
    width = heads * HEAD_SIZE
    group_width = QUERY_PER_KV * HEAD_SIZE
    span = REACH * tokens + ROWS
    scale = 1.0 / math.sqrt(HEAD_SIZE)
    exponent_scale = scale * math.log2(math.e)
    cross = section > 0
    others = sections - 1
    lent = heads // sections
    kept = heads - lent
    at_home = jnp.where(section == 0, 1, 0)
    has_before = block >= REACH
    has_after = block + REACH < blocks

    def block_rows(index):
        return pl.ds(index * tokens, tokens)

    def load_shared(head, kind):
        return pltpu.make_async_copy(
            projected_ref.at[:, pl.ds(kind * width + head * HEAD_SIZE, HEAD_SIZE)],
            window.at[head, kind, block_rows(REACH), :],
            load_sem.at[head, kind],
        )

    def load_group(head, kind):
        source, target = ((projected_ref, queries), (grad_out_ref, cotangents))[kind]
        return pltpu.make_async_copy(
            source.at[:, pl.ds(head * group_width, group_width)],
            target.at[head],
            load_sem.at[head, kind],
        )

    def lend_copy(index, kind, source):
        origin, target = ((projected_ref, queries), (grad_out_ref, cotangents))[kind]
        unit = index * others + source - 1
        return pltpu.make_async_remote_copy(
            src_ref=origin.at[:, pl.ds((kept + index) * group_width, group_width)],
            dst_ref=target.at[unit],
            send_sem=lend_send.at[index, kind],
            recv_sem=lend_recv.at[unit, kind],
            device_id={"section": 0, "ctx": block},
            device_id_type=MESH,
        )

    def owner_of(head):
        return (1 - head // kept) * (1 + lax.rem(head, others))

    def ring_copy(head, kind, way):
        target_place = lax.rem(place + 1 - 2 * way + sections, sections)
        own = window.at[head, kind, block_rows(REACH), :]
        return pltpu.make_async_remote_copy(
            src_ref=own,
            dst_ref=own,
            send_sem=ring_send.at[head, kind, way],
            recv_sem=ring_recv.at[head, kind],
            device_id={"section": ring_swap(target_place, sections), "ctx": block},
            device_id_type=MESH,
        )

    def ring_sends(kind, way):
        middle = sections // 2
        if way == 0:
            return place < middle if kind == 0 else place + 1 < middle
        above = lax.rem(place - 1 + sections, sections)
        starts = (place == 0) | (place > middle)
        return starts & (above > middle if kind == 0 else above >= middle)

    def ring_start(head, kind):
        for way in range(2):

            @pl.when(ring_sends(kind, way))
            def _():
                ring_copy(head, kind, way).start()

    def ring_sent(head):
        for kind in range(2):
            for way in range(2):

                @pl.when(ring_sends(kind, way))
                def _():
                    ring_copy(head, kind, way).wait_send()

    def to_block(source, target, send_sem, recv_sem, target_block):
        return pltpu.make_async_remote_copy(
            src_ref=source,
            dst_ref=target,
            send_sem=send_sem,
            recv_sem=recv_sem,
            device_id={"section": section, "ctx": target_block},
            device_id_type=MESH,
        )

    def hop_kv(head):
        return to_block(
            window.at[head, :, block_rows(REACH), :],
            window.at[head, :, block_rows(0), :],
            hop_kv_send.at[head],
            hop_kv_recv.at[head],
            block + REACH,
        )

    def pair_kv(head, source_block):
        return to_block(
            window.at[head, :, block_rows(source_block), :],
            window.at[head, :, block_rows(1), :],
            pair_kv_send.at[head],
            pair_kv_recv.at[head],
            partner,
        )

    def pair_grads(head):
        return to_block(
            grads.at[head, :, block_rows(1), :],
            pair_in.at[head],
            pair_send.at[head],
            pair_recv.at[head],
            partner,
        )

    def hop_grads(head, kind):
        return to_block(
            hop_out.at[head, kind],
            hop_in.at[head, kind],
            hop_send.at[head, kind],
            hop_recv.at[head, kind],
            block - REACH,
        )

    def part_copy(head, kind, source, target):
        return pltpu.make_async_remote_copy(
            src_ref=part_out.at[head, kind],
            dst_ref=part_in.at[head // others, source, kind],
            send_sem=part_send.at[head, kind],
            recv_sem=part_recv.at[head // others, source, kind],
            device_id={"section": target, "ctx": block},
            device_id_type=MESH,
        )

    def out_columns(head, kind):
        start = pl.multiple_of(kind * width + head * HEAD_SIZE, HEAD_SIZE)
        return out_ref.at[:, pl.ds(start, HEAD_SIZE)]

    def spread_copy(head, kind, target):
        return pltpu.make_async_remote_copy(
            src_ref=final_half.at[head, kind],
            dst_ref=out_columns(head, kind),
            send_sem=spread_send.at[head, target, kind],
            recv_sem=spread_recv.at[head, kind],
            device_id={"section": target, "ctx": block},
            device_id_type=MESH,
        )

    def store_copy(head, kind):
        return pltpu.make_async_copy(
            final_half.at[head, kind],
            out_columns(head, kind),
            store_sem.at[head, kind],
        )

    @pl.when(section == 0)
    def _():
        for head in range(heads):
            for kind in range(2):
                load_shared(head, kind).start()

    @pl.when(cross)
    def _():
        for head in range(kept):
            for kind in range(2):
                load_group(head, kind).start()

    barrier = pltpu.get_barrier_semaphore()
    for step in range(1, sections):
        pl.semaphore_signal(
            barrier,
            inc=1,
            device_id={"section": lax.rem(section + step, sections), "ctx": block},
            device_id_type=MESH,
        )
    pl.semaphore_signal(
        barrier, inc=1, device_id={"section": section, "ctx": partner}, device_id_type=MESH
    )

    @pl.when(has_before)
    def _():
        pl.semaphore_signal(
            barrier,
            inc=1,
            device_id={"section": section, "ctx": block - REACH},
            device_id_type=MESH,
        )

    @pl.when(has_after)
    def _():
        pl.semaphore_signal(
            barrier,
            inc=1,
            device_id={"section": section, "ctx": block + REACH},
            device_id_type=MESH,
        )

    before_count = jnp.where(has_before, 1, 0)
    after_count = jnp.where(has_after, 1, 0)
    pl.semaphore_wait(barrier, sections + before_count + after_count)

    def finish(head):
        own = block_rows(REACH)
        for kind in range(2):
            for source in range(1, sections):

                @pl.when(cross & (section != source))
                def _():
                    part_copy(head, kind, source, section).wait_recv()
                    grads[head, kind, own, :] += part_in[head // others, source, kind].astype(
                        jnp.float32
                    )

            total = grads[head, kind, own, :]
            if kind == 0:
                total = total * scale
            final_half[head, kind] = total.astype(jnp.bfloat16)
            store_copy(head, kind).start()
            for step in range(1, sections):
                spread_copy(head, kind, lax.rem(section + step, sections)).start()

    def pass_across(head):
        @pl.when(has_before & (odd == 1))
        def _():
            hop_kv(head).wait_recv()
            pair_kv(head, 0).start()

    def to_later(head):
        @pl.when(has_after)
        def _():
            hop_kv(head).start()

        @pl.when(odd == 0)
        def _():
            pair_kv(head, REACH).start()

    @pl.when(section == 0)
    def _():
        for head in range(min(3, kept)):
            for kind in range(2):
                load_shared(head, kind).wait()
                ring_start(head, kind)
        for head in range(min(3, kept), heads):
            for kind in range(2):
                load_shared(head, kind).wait()
        for head in range(kept, heads):
            to_later(head)

    @pl.when(cross)
    def _():
        for kind in range(2):
            lend_copy(0, kind, section).start()

    for index in range(tokens // ROWS):
        query_place = block * tokens + index * ROWS + lax.broadcasted_iota(
            jnp.int32, (8, ROWS), 1
        )
        start = jnp.zeros((8, ROWS), jnp.int32)
        end = 0
        for document in range(lengths_ref.shape[0]):
            end = end + lengths_ref[document]
            start = jnp.where(query_place >= end, end, start)
        key_place = (
            (block - REACH) * tokens
            + index * ROWS
            + lax.broadcasted_iota(jnp.int32, (span, ROWS), 0)
        )
        allowed = (key_place >= start[:1]) & (key_place <= query_place[:1])
        bias[index] = jnp.where(allowed, 0.0, MASKED_SCORE)

    @pl.loop(0, heads)
    def _(head):
        grads[head] = jnp.zeros(grads.shape[1:], jnp.float32)

        @pl.when(block < REACH)
        def _():
            window[head, :, block_rows(0), :] = jnp.zeros((2, tokens, HEAD_SIZE), jnp.bfloat16)

        @pl.when(block == 0)
        def _():
            window[head, :, block_rows(1), :] = jnp.zeros((2, tokens, HEAD_SIZE), jnp.bfloat16)

    @pl.when(section == 0)
    def _():
        for head in range(min(3, kept), kept):
            for kind in range(2):
                ring_start(head, kind)
        for head in range(kept, heads):
            pass_across(head)

    @pl.when(cross)
    def _():
        for head in range(kept):
            for kind in range(2):
                load_group(head, kind).wait()

    def pass_on(head):
        for kind in range(2):
            ring_copy(head, kind, 0).wait_recv()
            ring_start(head, kind)

        to_later(head)

    def compute(unit, head):
        chunks = span // ROWS

        def stacked(array, index):
            rows = pl.ds(index * ROWS, ROWS)
            return jnp.concatenate(
                [
                    array[unit, rows, member * HEAD_SIZE : (member + 1) * HEAD_SIZE]
                    for member in range(QUERY_PER_KV)
                ],
                axis=0,
            )

        def products(index):
            band = pl.ds(index * ROWS, span)
            scores = dot_last(window[head, 0, band, :], stacked(queries, index))
            top = jnp.full((8, QUERY_PER_KV * ROWS), -3e38, jnp.float32)
            for chunk in range(chunks):
                here = pl.ds(chunk * ROWS, ROWS)
                mask = bias[index, here, :]
                score = scores[chunk * ROWS : (chunk + 1) * ROWS] + jnp.concatenate(
                    [mask] * QUERY_PER_KV, axis=1
                )
                score_buf[index, here, :] = score
                top = jnp.maximum(top, folded(score, jnp.max))
            prob_grad_buf[index] = dot_last(
                window[head, 1, band, :], stacked(cotangents, index)
            )
            return jnp.max(top, axis=0, keepdims=True)

        def soften(index, top):
            total = jnp.zeros((8, QUERY_PER_KV * ROWS), jnp.float32)
            delta = jnp.zeros((8, QUERY_PER_KV * ROWS), jnp.float32)
            for chunk in range(chunks):
                here = pl.ds(chunk * ROWS, ROWS)
                power = jnp.exp2((score_buf[index, here, :] - top) * exponent_scale)
                score_buf[index, here, :] = power
                total = total + folded(power, jnp.sum)
                delta = delta + folded(power * prob_grad_buf[index, here, :], jnp.sum)
            inverse = 1.0 / jnp.sum(total, axis=0, keepdims=True)
            delta = jnp.sum(delta, axis=0, keepdims=True) * inverse
            for chunk in range(chunks):
                here = pl.ds(chunk * ROWS, ROWS)
                prob = score_buf[index, here, :] * inverse
                score_grad = prob * (prob_grad_buf[index, here, :] - delta)
                halves[index, 0, here, :] = score_grad.astype(jnp.bfloat16)
                halves[index, 1, here, :] = prob.astype(jnp.bfloat16)

        def accumulate(index):
            for kind, array in enumerate((queries, cotangents)):
                update = jnp.dot(
                    halves[index, kind],
                    stacked(array, index),
                    preferred_element_type=jnp.float32,
                )
                grads[head, kind, pl.ds(index * ROWS, span), :] += update

        count = tokens // ROWS
        tops = [products(0)]
        for index in range(count):
            if index + 1 < count:
                tops.append(products(index + 1))
            soften(index, tops[index])
            accumulate(index)

    def head_of(unit):
        return (1 - at_home) * unit + at_home * (kept + unit // others)

    def attend(unit):
        head = head_of(unit)
        first = cross | (lax.rem(unit, others) == 0)
        last = cross | (lax.rem(unit, others) == others - 1)

        @pl.when(section == 0)
        def _():
            for kind in range(2):
                lend_copy(unit // others, kind, 1 + lax.rem(unit, others)).wait_recv()

        @pl.when(first & has_before & (odd == 0))
        def _():
            hop_kv(head).wait_recv()

        @pl.when(first & (has_before | (odd == 1)))
        def _():
            pair_kv(head, REACH).wait_recv()

        compute(unit, head)

        @pl.when(last & (has_before | (odd == 1)))
        def _():
            pair_grads(head).start()

    def send_back(head):
        @pl.when(has_before)
        def _():
            @pl.when(odd == 1)
            def _():
                pair_grads(head).wait_recv()

            for kind in range(2):

                @pl.when(odd == 0)
                def _():
                    hop_out[head, kind] = grads[head, kind, block_rows(0), :].astype(jnp.bfloat16)

                @pl.when(odd == 1)
                def _():
                    hop_out[head, kind] = (
                        grads[head, kind, block_rows(0), :] + pair_in[head, kind]
                    ).astype(jnp.bfloat16)

                hop_grads(head, kind).start()

    def gather(head):
        owner = owner_of(head)

        @pl.when(odd == 0)
        def _():
            pair_grads(head).wait_recv()
            grads[head, :, block_rows(REACH), :] += pair_in[head]

        for kind in range(2):

            @pl.when(has_after)
            def _():
                hop_grads(head, kind).wait_recv()
                grads[head, kind, block_rows(REACH), :] += hop_in[head, kind].astype(jnp.float32)

            @pl.when(owner != section)
            def _():
                part_out[head, kind] = grads[head, kind, block_rows(REACH), :].astype(jnp.bfloat16)
                part_copy(head, kind, section, owner).start()

    @pl.loop(0, kept + AHEAD + 4)
    def _(step):
        def stage(lag, run):
            unit = step - lag

            @pl.when((unit >= 0) & (unit < kept))
            def _():
                run(unit)

        def when_summed(run):
            def staged(unit):
                @pl.when(cross | (lax.rem(unit, others) == others - 1))
                def _():
                    run(head_of(unit))

            return staged

        def when_cross(run):
            def staged(unit):
                @pl.when(cross)
                def _():
                    run(unit)

            return staged

        def finish_own(head):
            @pl.when(owner_of(head) == section)
            def _():
                finish(head)

        stage(0, when_cross(pass_on))
        stage(1, when_cross(pass_across))
        for index in range(1, lent):

            @pl.when(cross & (step == AHEAD + index - 1))
            def _():
                for kind in range(2):
                    lend_copy(index, kind, section).start()

        stage(AHEAD, attend)
        stage(AHEAD + 1, when_summed(send_back))
        stage(AHEAD + 2, when_summed(gather))
        stage(AHEAD + 3, when_summed(finish_own))

    @pl.loop(0, heads)
    def _(head):
        owner = owner_of(head)
        home = head // kept
        for kind in range(2):

            @pl.when(owner == section)
            def _():
                store_copy(head, kind).wait()
                for step in range(1, sections):
                    spread_copy(head, kind, lax.rem(section + step, sections)).wait_send()

            @pl.when(owner != section)
            def _():
                spread_copy(head, kind, owner).wait_recv()


        @pl.when(home == 0)
        def _():
            ring_sent(head)

        @pl.when(cross & (home == 1))
        def _():
            for kind in range(2):
                lend_copy(head - kept, kind, section).wait_send()

        @pl.when(home == at_home)
        def _():
            @pl.when(has_after)
            def _():
                hop_kv(head).wait_send()

            @pl.when(has_before | (odd == 0))
            def _():
                pair_kv(head, REACH).wait_send()

            @pl.when(has_before | (odd == 1))
            def _():
                pair_grads(head).wait_send()

            @pl.when(has_before)
            def _():
                for kind in range(2):
                    hop_grads(head, kind).wait_send()

            @pl.when(owner != section)
            def _():
                for kind in range(2):
                    part_copy(head, kind, section, owner).wait_send()


def on_device(projected, grad_out, doc_lengths):
    sections = lax.axis_size("section")
    blocks = lax.axis_size("ctx")
    tokens = projected.shape[1]
    heads = KV_HEAD_COUNT
    lent = heads // sections
    kept = heads - lent
    span = REACH * tokens + ROWS
    window_rows = (REACH + 1) * tokens
    group_width = QUERY_PER_KV * HEAD_SIZE
    bf16, f32 = jnp.bfloat16, jnp.float32
    dma = pltpu.SemaphoreType.DMA
    return pl.pallas_call(
        functools.partial(kernel, sections, blocks),
        out_shape=jax.ShapeDtypeStruct((tokens, 2 * heads * HEAD_SIZE), bf16),
        in_specs=[
            pl.BlockSpec(memory_space=pltpu.SMEM),
            pl.BlockSpec(memory_space=pl.ANY),
            pl.BlockSpec(memory_space=pl.ANY),
        ],
        out_specs=pl.BlockSpec(memory_space=pl.ANY),
        scratch_shapes=[
            pltpu.VMEM((kept, tokens, group_width), bf16),
            pltpu.VMEM((kept, tokens, group_width), bf16),
            pltpu.VMEM((heads, 2, window_rows, HEAD_SIZE), bf16),
            pltpu.VMEM((tokens // ROWS, span, ROWS), f32),
            pltpu.VMEM((tokens // ROWS, span, QUERY_PER_KV * ROWS), f32),
            pltpu.VMEM((tokens // ROWS, span, QUERY_PER_KV * ROWS), f32),
            pltpu.VMEM((tokens // ROWS, 2, span, QUERY_PER_KV * ROWS), bf16),
            pltpu.VMEM((heads, 2, window_rows, HEAD_SIZE), f32),
            pltpu.VMEM((heads, 2, tokens, HEAD_SIZE), f32),
            pltpu.VMEM((heads, 2, tokens, HEAD_SIZE), bf16),
            pltpu.VMEM((heads, 2, tokens, HEAD_SIZE), bf16),
            pltpu.VMEM((heads, 2, tokens, HEAD_SIZE), bf16),
            pltpu.VMEM((lent, sections, 2, tokens, HEAD_SIZE), bf16),
            pltpu.VMEM((heads, 2, tokens, HEAD_SIZE), bf16),
            dma((heads, 2)),
            dma((lent, 2)),
            dma((kept, 2)),
            dma((heads, 2, 2)),
            dma((heads, 2)),
            dma((heads,)),
            dma((heads,)),
            dma((heads,)),
            dma((heads,)),
            dma((heads,)),
            dma((heads,)),
            dma((heads, 2)),
            dma((heads, 2)),
            dma((heads, 2)),
            dma((lent, sections, 2)),
            dma((heads, sections, 2)),
            dma((heads, 2)),
            dma((heads, 2)),
        ],
        compiler_params=pltpu.CompilerParams(
            collective_id=0, has_side_effects=True, vmem_limit_bytes=56 * 1024 * 1024
        ),
        cost_estimate=pl.CostEstimate(
            flops=10 * heads * tokens * group_width * span // 1,
            bytes_accessed=16 * tokens * heads * group_width,
            transcendentals=heads * QUERY_PER_KV * tokens * span,
        ),
    )(doc_lengths, projected[0], grad_out[0]).astype(f32)


def solution(mesh):
    return jax.shard_map(
        on_device,
        mesh=mesh,
        in_specs=(P("section", "ctx", None), P("section", "ctx", None), P()),
        out_specs=P("ctx", None),
        check_vma=False,
    )
```

```python
import functools
import math

import jax
import jax.numpy as jnp
from jax import lax
from jax.experimental import pallas as pl
from jax.experimental.pallas import tpu as pltpu
from jax.sharding import PartitionSpec as P

HEAD_SIZE = 128
KV_HEAD_COUNT = 8
QUERY_PER_KV = 3
REACH = 2
ROWS = 128
AHEAD = 2
MASKED_SCORE = -1e30
MESH = pl.DeviceIdType.MESH


def ring_swap(place, sections):
    half = sections // 2
    back = place // half
    return place * (1 - back) + back * (half + sections - 1 - place)


def dot_last(left, right):
    return lax.dot_general(
        left, right, (((1,), (1,)), ((), ())), preferred_element_type=jnp.float32
    )


def folded(value, reduce):
    return reduce(value.reshape(-1, 8, value.shape[-1]), axis=0)


def kernel(
    sections,
    blocks,
    lengths_ref,
    projected_ref,
    grad_out_ref,
    out_ref,
    queries,
    cotangents,
    window,
    bias,
    score_buf,
    prob_grad_buf,
    halves,
    grads,
    pair_in,
    hop_out,
    hop_in,
    part_out,
    part_in,
    final_half,
    load_sem,
    lend_send,
    lend_recv,
    ring_send,
    ring_recv,
    hop_kv_send,
    hop_kv_recv,
    pair_kv_send,
    pair_kv_recv,
    pair_send,
    pair_recv,
    hop_send,
    hop_recv,
    part_send,
    part_recv,
    spread_send,
    spread_recv,
    store_sem,
):
    section = lax.axis_index("section")
    block = lax.axis_index("ctx")
    odd = lax.rem(block, 2)
    partner = block + 1 - 2 * odd
    place = ring_swap(section, sections)
    heads = KV_HEAD_COUNT
    tokens = out_ref.shape[0]
    width = heads * HEAD_SIZE
    group_width = QUERY_PER_KV * HEAD_SIZE
    span = REACH * tokens + ROWS
    scale = 1.0 / math.sqrt(HEAD_SIZE)
    exponent_scale = scale * math.log2(math.e)
    cross = section > 0
    others = sections - 1
    lent = heads // sections
    kept = heads - lent
    at_home = jnp.where(section == 0, 1, 0)
    has_before = block >= REACH
    has_after = block + REACH < blocks

    def block_rows(index):
        return pl.ds(index * tokens, tokens)

    def load_shared(head, kind):
        return pltpu.make_async_copy(
            projected_ref.at[:, pl.ds(kind * width + head * HEAD_SIZE, HEAD_SIZE)],
            window.at[head, kind, block_rows(REACH), :],
            load_sem.at[head, kind],
        )

    def load_group(head, kind):
        source, target = ((projected_ref, queries), (grad_out_ref, cotangents))[kind]
        return pltpu.make_async_copy(
            source.at[:, pl.ds(head * group_width, group_width)],
            target.at[head],
            load_sem.at[head, kind],
        )

    def lend_copy(index, kind, source):
        origin, target = ((projected_ref, queries), (grad_out_ref, cotangents))[kind]
        unit = index * others + source - 1
        return pltpu.make_async_remote_copy(
            src_ref=origin.at[:, pl.ds((kept + index) * group_width, group_width)],
            dst_ref=target.at[unit],
            send_sem=lend_send.at[index, kind],
            recv_sem=lend_recv.at[unit, kind],
            device_id={"section": 0, "ctx": block},
            device_id_type=MESH,
        )

    def owner_of(head):
        return (1 - head // kept) * (1 + lax.rem(head, others))

    def ring_copy(head, kind, way):
        target_place = lax.rem(place + 1 - 2 * way + sections, sections)
        own = window.at[head, kind, block_rows(REACH), :]
        return pltpu.make_async_remote_copy(
            src_ref=own,
            dst_ref=own,
            send_sem=ring_send.at[head, kind, way],
            recv_sem=ring_recv.at[head, kind],
            device_id={"section": ring_swap(target_place, sections), "ctx": block},
            device_id_type=MESH,
        )

    def ring_sends(kind, way):
        middle = sections // 2
        if way == 0:
            return place < middle if kind == 0 else place + 1 < middle
        above = lax.rem(place - 1 + sections, sections)
        starts = (place == 0) | (place > middle)
        return starts & (above > middle if kind == 0 else above >= middle)

    def ring_start(head, kind):
        for way in range(2):

            @pl.when(ring_sends(kind, way))
            def _():
                ring_copy(head, kind, way).start()

    def ring_sent(head):
        for kind in range(2):
            for way in range(2):

                @pl.when(ring_sends(kind, way))
                def _():
                    ring_copy(head, kind, way).wait_send()

    def to_block(source, target, send_sem, recv_sem, target_block):
        return pltpu.make_async_remote_copy(
            src_ref=source,
            dst_ref=target,
            send_sem=send_sem,
            recv_sem=recv_sem,
            device_id={"section": section, "ctx": target_block},
            device_id_type=MESH,
        )

    def hop_kv(head):
        return to_block(
            window.at[head, :, block_rows(REACH), :],
            window.at[head, :, block_rows(0), :],
            hop_kv_send.at[head],
            hop_kv_recv.at[head],
            block + REACH,
        )

    def pair_kv(head, source_block):
        return to_block(
            window.at[head, :, block_rows(source_block), :],
            window.at[head, :, block_rows(1), :],
            pair_kv_send.at[head],
            pair_kv_recv.at[head],
            partner,
        )

    def pair_grads(head):
        return to_block(
            grads.at[head, :, block_rows(1), :],
            pair_in.at[head],
            pair_send.at[head],
            pair_recv.at[head],
            partner,
        )

    def hop_grads(head, kind):
        return to_block(
            hop_out.at[head, kind],
            hop_in.at[head, kind],
            hop_send.at[head, kind],
            hop_recv.at[head, kind],
            block - REACH,
        )

    def part_copy(head, kind, source, target):
        return pltpu.make_async_remote_copy(
            src_ref=part_out.at[head, kind],
            dst_ref=part_in.at[head // others, source, kind],
            send_sem=part_send.at[head, kind],
            recv_sem=part_recv.at[head // others, source, kind],
            device_id={"section": target, "ctx": block},
            device_id_type=MESH,
        )

    def out_columns(head, kind):
        start = pl.multiple_of(kind * width + head * HEAD_SIZE, HEAD_SIZE)
        return out_ref.at[:, pl.ds(start, HEAD_SIZE)]

    def spread_copy(head, kind, target):
        return pltpu.make_async_remote_copy(
            src_ref=final_half.at[head, kind],
            dst_ref=out_columns(head, kind),
            send_sem=spread_send.at[head, target, kind],
            recv_sem=spread_recv.at[head, kind],
            device_id={"section": target, "ctx": block},
            device_id_type=MESH,
        )

    def store_copy(head, kind):
        return pltpu.make_async_copy(
            final_half.at[head, kind],
            out_columns(head, kind),
            store_sem.at[head, kind],
        )

    @pl.when(section == 0)
    def _():
        for head in range(heads):
            for kind in range(2):
                load_shared(head, kind).start()

    @pl.when(cross)
    def _():
        for head in range(kept):
            for kind in range(2):
                load_group(head, kind).start()

    barrier = pltpu.get_barrier_semaphore()
    for step in range(1, sections):
        pl.semaphore_signal(
            barrier,
            inc=1,
            device_id={"section": lax.rem(section + step, sections), "ctx": block},
            device_id_type=MESH,
        )
    pl.semaphore_signal(
        barrier, inc=1, device_id={"section": section, "ctx": partner}, device_id_type=MESH
    )

    @pl.when(has_before)
    def _():
        pl.semaphore_signal(
            barrier,
            inc=1,
            device_id={"section": section, "ctx": block - REACH},
            device_id_type=MESH,
        )

    @pl.when(has_after)
    def _():
        pl.semaphore_signal(
            barrier,
            inc=1,
            device_id={"section": section, "ctx": block + REACH},
            device_id_type=MESH,
        )

    before_count = jnp.where(has_before, 1, 0)
    after_count = jnp.where(has_after, 1, 0)
    pl.semaphore_wait(barrier, sections + before_count + after_count)

    def finish(head):
        own = block_rows(REACH)
        for kind in range(2):
            for source in range(1, sections):

                @pl.when(cross & (section != source))
                def _():
                    part_copy(head, kind, source, section).wait_recv()
                    grads[head, kind, own, :] += part_in[head // others, source, kind].astype(
                        jnp.float32
                    )

            total = grads[head, kind, own, :]
            if kind == 0:
                total = total * scale
            final_half[head, kind] = total.astype(jnp.bfloat16)
            store_copy(head, kind).start()
            for step in range(1, sections):
                spread_copy(head, kind, lax.rem(section + step, sections)).start()

    def pass_across(head):
        @pl.when(has_before & (odd == 1))
        def _():
            hop_kv(head).wait_recv()
            pair_kv(head, 0).start()

    def to_later(head):
        @pl.when(has_after)
        def _():
            hop_kv(head).start()

        @pl.when(odd == 0)
        def _():
            pair_kv(head, REACH).start()

    @pl.when(section == 0)
    def _():
        for head in range(min(3, kept)):
            for kind in range(2):
                load_shared(head, kind).wait()
                ring_start(head, kind)
        for head in range(min(3, kept), heads):
            for kind in range(2):
                load_shared(head, kind).wait()
        for head in range(kept, heads):
            to_later(head)

    @pl.when(cross)
    def _():
        for kind in range(2):
            lend_copy(0, kind, section).start()

    for index in range(tokens // ROWS):
        query_place = block * tokens + index * ROWS + lax.broadcasted_iota(
            jnp.int32, (8, ROWS), 1
        )
        start = jnp.zeros((8, ROWS), jnp.int32)
        end = 0
        for document in range(lengths_ref.shape[0]):
            end = end + lengths_ref[document]
            start = jnp.where(query_place >= end, end, start)
        key_place = (
            (block - REACH) * tokens
            + index * ROWS
            + lax.broadcasted_iota(jnp.int32, (span, ROWS), 0)
        )
        allowed = (key_place >= start[:1]) & (key_place <= query_place[:1])
        bias[index] = jnp.where(allowed, 0.0, MASKED_SCORE)

    @pl.loop(0, heads)
    def _(head):
        grads[head] = jnp.zeros(grads.shape[1:], jnp.float32)

        @pl.when(block < REACH)
        def _():
            window[head, :, block_rows(0), :] = jnp.zeros((2, tokens, HEAD_SIZE), jnp.bfloat16)

        @pl.when(block == 0)
        def _():
            window[head, :, block_rows(1), :] = jnp.zeros((2, tokens, HEAD_SIZE), jnp.bfloat16)

    @pl.when(section == 0)
    def _():
        for head in range(min(3, kept), kept):
            for kind in range(2):
                ring_start(head, kind)
        for head in range(kept, heads):
            pass_across(head)

    @pl.when(cross)
    def _():
        for head in range(kept):
            for kind in range(2):
                load_group(head, kind).wait()

    def pass_on(head):
        for kind in range(2):
            ring_copy(head, kind, 0).wait_recv()
            ring_start(head, kind)

        to_later(head)

    def compute(unit, head):
        chunks = span // ROWS

        def stacked(array, index):
            rows = pl.ds(index * ROWS, ROWS)
            return jnp.concatenate(
                [
                    array[unit, rows, member * HEAD_SIZE : (member + 1) * HEAD_SIZE]
                    for member in range(QUERY_PER_KV)
                ],
                axis=0,
            )

        def products(index):
            band = pl.ds(index * ROWS, span)
            scores = dot_last(window[head, 0, band, :], stacked(queries, index))
            top = jnp.full((8, QUERY_PER_KV * ROWS), -3e38, jnp.float32)
            for chunk in range(chunks):
                here = pl.ds(chunk * ROWS, ROWS)
                mask = bias[index, here, :]
                score = scores[chunk * ROWS : (chunk + 1) * ROWS] + jnp.concatenate(
                    [mask] * QUERY_PER_KV, axis=1
                )
                score_buf[index, here, :] = score
                top = jnp.maximum(top, folded(score, jnp.max))
            prob_grad_buf[index] = dot_last(
                window[head, 1, band, :], stacked(cotangents, index)
            )
            return jnp.max(top, axis=0, keepdims=True)

        def soften(index, top):
            total = jnp.zeros((8, QUERY_PER_KV * ROWS), jnp.float32)
            delta = jnp.zeros((8, QUERY_PER_KV * ROWS), jnp.float32)
            for chunk in range(chunks):
                here = pl.ds(chunk * ROWS, ROWS)
                power = jnp.exp2((score_buf[index, here, :] - top) * exponent_scale)
                score_buf[index, here, :] = power
                total = total + folded(power, jnp.sum)
                delta = delta + folded(power * prob_grad_buf[index, here, :], jnp.sum)
            inverse = 1.0 / jnp.sum(total, axis=0, keepdims=True)
            delta = jnp.sum(delta, axis=0, keepdims=True) * inverse
            for chunk in range(chunks):
                here = pl.ds(chunk * ROWS, ROWS)
                prob = score_buf[index, here, :] * inverse
                score_grad = prob * (prob_grad_buf[index, here, :] - delta)
                halves[index, 0, here, :] = score_grad.astype(jnp.bfloat16)
                halves[index, 1, here, :] = prob.astype(jnp.bfloat16)

        def accumulate(index):
            for kind, array in enumerate((queries, cotangents)):
                update = jnp.dot(
                    halves[index, kind],
                    stacked(array, index),
                    preferred_element_type=jnp.float32,
                )
                grads[head, kind, pl.ds(index * ROWS, span), :] += update

        count = tokens // ROWS
        tops = [products(0)]
        for index in range(count):
            if index + 1 < count:
                tops.append(products(index + 1))
            if index:
                accumulate(index - 1)
            soften(index, tops[index])
        accumulate(count - 1)

    def head_of(unit):
        return (1 - at_home) * unit + at_home * (kept + unit // others)

    def attend(unit):
        head = head_of(unit)
        first = cross | (lax.rem(unit, others) == 0)
        last = cross | (lax.rem(unit, others) == others - 1)

        @pl.when(section == 0)
        def _():
            for kind in range(2):
                lend_copy(unit // others, kind, 1 + lax.rem(unit, others)).wait_recv()

        @pl.when(first & has_before & (odd == 0))
        def _():
            hop_kv(head).wait_recv()

        @pl.when(first & (has_before | (odd == 1)))
        def _():
            pair_kv(head, REACH).wait_recv()

        compute(unit, head)

        @pl.when(last & (has_before | (odd == 1)))
        def _():
            pair_grads(head).start()

    def send_back(head):
        @pl.when(has_before)
        def _():
            @pl.when(odd == 1)
            def _():
                pair_grads(head).wait_recv()

            for kind in range(2):

                @pl.when(odd == 0)
                def _():
                    hop_out[head, kind] = grads[head, kind, block_rows(0), :].astype(jnp.bfloat16)

                @pl.when(odd == 1)
                def _():
                    hop_out[head, kind] = (
                        grads[head, kind, block_rows(0), :] + pair_in[head, kind]
                    ).astype(jnp.bfloat16)

                hop_grads(head, kind).start()

    def gather(head):
        owner = owner_of(head)

        @pl.when(odd == 0)
        def _():
            pair_grads(head).wait_recv()
            grads[head, :, block_rows(REACH), :] += pair_in[head]

        for kind in range(2):

            @pl.when(has_after)
            def _():
                hop_grads(head, kind).wait_recv()
                grads[head, kind, block_rows(REACH), :] += hop_in[head, kind].astype(jnp.float32)

            @pl.when(owner != section)
            def _():
                part_out[head, kind] = grads[head, kind, block_rows(REACH), :].astype(jnp.bfloat16)
                part_copy(head, kind, section, owner).start()

    @pl.loop(0, kept + AHEAD + 4)
    def _(step):
        def stage(lag, run):
            unit = step - lag

            @pl.when((unit >= 0) & (unit < kept))
            def _():
                run(unit)

        def when_summed(run):
            def staged(unit):
                @pl.when(cross | (lax.rem(unit, others) == others - 1))
                def _():
                    run(head_of(unit))

            return staged

        def when_cross(run):
            def staged(unit):
                @pl.when(cross)
                def _():
                    run(unit)

            return staged

        def finish_own(head):
            @pl.when(owner_of(head) == section)
            def _():
                finish(head)

        stage(0, when_cross(pass_on))
        stage(1, when_cross(pass_across))
        for index in range(1, lent):

            @pl.when(cross & (step == AHEAD + index - 1))
            def _():
                for kind in range(2):
                    lend_copy(index, kind, section).start()

        stage(AHEAD, attend)
        stage(AHEAD + 1, when_summed(send_back))
        stage(AHEAD + 2, when_summed(gather))
        stage(AHEAD + 3, when_summed(finish_own))

    @pl.loop(0, heads)
    def _(head):
        owner = owner_of(head)
        home = head // kept
        for kind in range(2):

            @pl.when(owner == section)
            def _():
                store_copy(head, kind).wait()
                for step in range(1, sections):
                    spread_copy(head, kind, lax.rem(section + step, sections)).wait_send()

            @pl.when(owner != section)
            def _():
                spread_copy(head, kind, owner).wait_recv()


        @pl.when(home == 0)
        def _():
            ring_sent(head)

        @pl.when(cross & (home == 1))
        def _():
            for kind in range(2):
                lend_copy(head - kept, kind, section).wait_send()

        @pl.when(home == at_home)
        def _():
            @pl.when(has_after)
            def _():
                hop_kv(head).wait_send()

            @pl.when(has_before | (odd == 0))
            def _():
                pair_kv(head, REACH).wait_send()

            @pl.when(has_before | (odd == 1))
            def _():
                pair_grads(head).wait_send()

            @pl.when(has_before)
            def _():
                for kind in range(2):
                    hop_grads(head, kind).wait_send()

            @pl.when(owner != section)
            def _():
                for kind in range(2):
                    part_copy(head, kind, section, owner).wait_send()


def on_device(projected, grad_out, doc_lengths):
    sections = lax.axis_size("section")
    blocks = lax.axis_size("ctx")
    tokens = projected.shape[1]
    heads = KV_HEAD_COUNT
    lent = heads // sections
    kept = heads - lent
    span = REACH * tokens + ROWS
    window_rows = (REACH + 1) * tokens
    group_width = QUERY_PER_KV * HEAD_SIZE
    bf16, f32 = jnp.bfloat16, jnp.float32
    dma = pltpu.SemaphoreType.DMA
    return pl.pallas_call(
        functools.partial(kernel, sections, blocks),
        out_shape=jax.ShapeDtypeStruct((tokens, 2 * heads * HEAD_SIZE), bf16),
        in_specs=[
            pl.BlockSpec(memory_space=pltpu.SMEM),
            pl.BlockSpec(memory_space=pl.ANY),
            pl.BlockSpec(memory_space=pl.ANY),
        ],
        out_specs=pl.BlockSpec(memory_space=pl.ANY),
        scratch_shapes=[
            pltpu.VMEM((kept, tokens, group_width), bf16),
            pltpu.VMEM((kept, tokens, group_width), bf16),
            pltpu.VMEM((heads, 2, window_rows, HEAD_SIZE), bf16),
            pltpu.VMEM((tokens // ROWS, span, ROWS), f32),
            pltpu.VMEM((tokens // ROWS, span, QUERY_PER_KV * ROWS), f32),
            pltpu.VMEM((tokens // ROWS, span, QUERY_PER_KV * ROWS), f32),
            pltpu.VMEM((tokens // ROWS, 2, span, QUERY_PER_KV * ROWS), bf16),
            pltpu.VMEM((heads, 2, window_rows, HEAD_SIZE), f32),
            pltpu.VMEM((heads, 2, tokens, HEAD_SIZE), f32),
            pltpu.VMEM((heads, 2, tokens, HEAD_SIZE), bf16),
            pltpu.VMEM((heads, 2, tokens, HEAD_SIZE), bf16),
            pltpu.VMEM((heads, 2, tokens, HEAD_SIZE), bf16),
            pltpu.VMEM((lent, sections, 2, tokens, HEAD_SIZE), bf16),
            pltpu.VMEM((heads, 2, tokens, HEAD_SIZE), bf16),
            dma((heads, 2)),
            dma((lent, 2)),
            dma((kept, 2)),
            dma((heads, 2, 2)),
            dma((heads, 2)),
            dma((heads,)),
            dma((heads,)),
            dma((heads,)),
            dma((heads,)),
            dma((heads,)),
            dma((heads,)),
            dma((heads, 2)),
            dma((heads, 2)),
            dma((heads, 2)),
            dma((lent, sections, 2)),
            dma((heads, sections, 2)),
            dma((heads, 2)),
            dma((heads, 2)),
        ],
        compiler_params=pltpu.CompilerParams(
            collective_id=0, has_side_effects=True, vmem_limit_bytes=56 * 1024 * 1024
        ),
        cost_estimate=pl.CostEstimate(
            flops=10 * heads * tokens * group_width * span // 1,
            bytes_accessed=16 * tokens * heads * group_width,
            transcendentals=heads * QUERY_PER_KV * tokens * span,
        ),
    )(doc_lengths, projected[0], grad_out[0]).astype(f32)


def solution(mesh):
    return jax.shard_map(
        on_device,
        mesh=mesh,
        in_specs=(P("section", "ctx", None), P("section", "ctx", None), P()),
        out_specs=P("ctx", None),
        check_vma=False,
    )
```
